32 devices in a mesh: dp: 16 (over z, y, x), seq: 2 (over core).
Axes of the slice: x: 2, y: 2, z: 4, core: 2. Of those that a mesh axis runs over, the one named last changes fastest.
Arguments:
- inputs: bfloat16 [16, 512, 768], P('dp', 'seq'), may hold values from -6 to 6
- pair_lengths: int32 [16, 8], P('dp'), may hold values from 1 to 175, as said below
- w_query: bfloat16 [768, 768], replicated, may hold values from -0.21875 to 0.21875
- w_key: bfloat16 [768, 768], replicated, may hold values from -0.21875 to 0.21875
- w_value: bfloat16 [768, 768], replicated, may hold values from -0.21875 to 0.21875
- w_out: bfloat16 [768, 768], replicated, may hold values from -0.625 to 0.625
- w_up: bfloat16 [768, 3072], replicated, may hold values from -0.21875 to 0.21875
- w_down: bfloat16 [3072, 768], replicated, may hold values from -0.15625 to 0.15625
- a_query: bfloat16 [768, 8], replicated, may hold values from -0.21875 to 0.21875
- b_query: bfloat16 [8, 768], replicated, may hold values from -1 to 1
- a_value: bfloat16 [768, 8], replicated, may hold values from -0.21875 to 0.21875
- b_value: bfloat16 [8, 768], replicated, may hold values from -1 to 1
- gain_one: float32 [768], replicated, may hold values from 0.5 to 1.5
- shift_one: float32 [768], replicated, may hold values from -3 to 3
- gain_two: float32 [768], replicated, may hold values from 0.5 to 1.5
- shift_two: float32 [768], replicated, may hold values from -3 to 3
- cotangent: bfloat16 [16, 512, 768], P('dp', 'seq'), may hold values from -6 to 6
Outputs:
- output: bfloat16 [16, 512, 768], P('dp', 'seq')
- grad_inputs: float32 [16, 512, 768], P('dp', 'seq')
- grad_a_query: float32 [768, 8], replicated
- grad_b_query: float32 [8, 768], replicated
- grad_a_value: float32 [768, 8], replicated
- grad_b_value: float32 [8, 768], replicated
- grad_gain_one: float32 [768], replicated
- grad_shift_one: float32 [768], replicated
- grad_gain_two: float32 [768], replicated
- grad_shift_two: float32 [768], replicated
The draws below stay inside these ranges and needn't reach their ends.
Inputs may be any that keep to these rules, and one draw needn't show every extreme that they name: `pair_lengths`: each row's entries sum to at least 384 and at most 512; positions past the sum are padding. Some row in every draw has no padding and a last pair of the largest length.
All inputs are finite; a program needn't handle non-finite values.
Results may differ from the reference program's by a relative error of at most 0.015.
Values may be sent and summed in bfloat16 or wider, within the bound.
No kernel may reach another device: no remote copies, remote signals or barrier semaphores. Data moves between devices by JAX's collectives and lax.ppermute only.
A program may use at most 128 MiB of HBM per device.

```python
import math
import jax
import jax.numpy as jnp
from jax import lax

D = 768
H = 12
FF = 3072
DH = 64
R = 8
LEN = 512
PAIRS = 8
SEQUENCES = 16


def draw_pair_lengths(key, part):
    key = jax.random.fold_in(key, 7)
    pad_key, cut_key, row_key = jax.random.split(key, 3)
    width_bin = 3 * LEN // 4 // PAIRS
    chosen_row = jax.random.randint(row_key, (), 0, SEQUENCES, dtype=jnp.int32)
    row_numbers = jnp.arange(SEQUENCES, dtype=jnp.int32)[:, None]
    padding = jax.random.randint(pad_key, (SEQUENCES, 1), 0, LEN // 4 + 1, dtype=jnp.int32)
    padding = jnp.where(row_numbers == chosen_row, 0, padding)
    offsets = jax.random.randint(cut_key, (SEQUENCES, PAIRS - 1), 1, width_bin, dtype=jnp.int32)
    last_column = jnp.arange(PAIRS - 1, dtype=jnp.int32)[None, :] == PAIRS - 2
    offsets = jnp.where(jnp.logical_and(row_numbers == chosen_row, last_column), 1, offsets)
    cut_points = (jnp.arange(1, PAIRS, dtype=jnp.int32) * width_bin)[None, :] + offsets
    cut_points = jnp.where(cut_points == LEN // 2, cut_points - 1, cut_points)
    used_length = LEN - padding
    starts = jnp.concatenate([jnp.zeros((SEQUENCES, 1), jnp.int32), cut_points], axis=1)
    stop_points = jnp.concatenate([cut_points, used_length], axis=1)
    return (stop_points - starts).astype(jnp.int32)


def shard_levels(own_key, dims, pieces, least, largest):
    loudness, own = 1.0, jax.random.fold_in(own_key, 6)
    for axis_at, parts in pieces:
        steps = jnp.exp(jax.random.uniform(jax.random.fold_in(own, axis_at), (parts,), jnp.float32, least / len(pieces), largest / len(pieces)))
        loudness = loudness * jnp.repeat(steps, dims[axis_at] // parts).reshape([-1 if axis == axis_at else 1 for axis in range(len(dims))])
    return loudness


def bell_draw(key, shape, deviation, limit, cuts=(), kind=jnp.bfloat16):
    values = jax.random.normal(key, shape, jnp.float32) * deviation
    if len(cuts) > 0:
        values = shard_levels(key, shape, cuts, -0.22, 0.18) * values
    return jnp.clip(values, min=-limit, max=limit).astype(kind)


def setup_inputs(seed: int = 0) -> dict:
    arg_keys = jax.random.split(jax.random.key(seed), 18)
    inputs = bell_draw(arg_keys[0], (SEQUENCES, LEN, D), 1.0, 6.0, ((0, 16), (1, 2)))
    pair_lengths = draw_pair_lengths(jax.random.fold_in(arg_keys[17], 71), 0)
    w_query = bell_draw(arg_keys[2], (D, D), D ** -0.5, 0.21875)
    w_key = bell_draw(arg_keys[3], (D, D), D ** -0.5, 0.21875)
    w_value = bell_draw(arg_keys[4], (D, D), D ** -0.5, 0.21875)
    w_out = bell_draw(arg_keys[5], (D, D), (D // 8) ** -0.5, 0.625)
    w_up = bell_draw(arg_keys[6], (D, FF), D ** -0.5, 0.21875)
    w_down = bell_draw(arg_keys[7], (FF, D), (FF // 2) ** -0.5, 0.15625)
    a_query = bell_draw(arg_keys[8], (D, R), D ** -0.5, 0.21875)
    b_query = bell_draw(arg_keys[9], (R, D), (4 * R) ** -0.5, 1.0)
    a_value = bell_draw(arg_keys[10], (D, R), D ** -0.5, 0.21875)
    b_value = bell_draw(arg_keys[11], (R, D), (4 * R) ** -0.5, 1.0)
    gain_one = jnp.clip(1.0 + 0.1 * jax.random.normal(arg_keys[12], (D,), jnp.float32), 0.5, 1.5)
    shift_one = bell_draw(arg_keys[13], (D,), 0.5, 3.0, (), jnp.float32)
    gain_two = jnp.clip(1.0 + 0.1 * jax.random.normal(arg_keys[14], (D,), jnp.float32), 0.5, 1.5)
    shift_two = bell_draw(arg_keys[15], (D,), 0.5, 3.0, (), jnp.float32)
    cotangent = bell_draw(arg_keys[16], (SEQUENCES, LEN, D), 1.0, 6.0, ((0, 16), (1, 2)))
    return {"inputs": inputs, "pair_lengths": pair_lengths, "w_query": w_query, "w_key": w_key, "w_value": w_value, "w_out": w_out, "w_up": w_up, "w_down": w_down, "a_query": a_query, "b_query": b_query, "a_value": a_value, "b_value": b_value, "gain_one": gain_one, "shift_one": shift_one, "gain_two": gain_two, "shift_two": shift_two, "cotangent": cotangent}


@jax.custom_vjp
def low(v):
    return lax.optimization_barrier(v.astype(jnp.bfloat16)).astype(jnp.float32)

@jax.custom_vjp
def low_back(v):
    return v

def low_keep(v):
    return (low(v), None)

def low_pass(kept, grad):
    return (grad,)

def back_keep(v):
    return (v, None)

def back_low(kept, grad):
    return (low(grad),)
low.defvjp(low_keep, low_pass)
low_back.defvjp(back_keep, back_low)
norm_epsilon = 1e-05

def segment_ids(lengths, span_length):
    pair_ends = jnp.cumsum(lengths, axis=-1).astype(jnp.int32)
    places = jnp.arange(span_length, dtype=jnp.int32)
    return lax.optimization_barrier(jnp.sum((places[None, :, None] >= pair_ends[:, None, :]).astype(jnp.int32), axis=-1))

def norm_rows(values, gain_vec, shift_vec):
    centred = values - lax.optimization_barrier(jnp.mean(values, axis=-1, keepdims=True))
    variance = lax.optimization_barrier(jnp.mean(centred * centred, axis=-1, keepdims=True))
    return centred * lax.rsqrt(variance + norm_epsilon) * gain_vec + shift_vec

def project(values, weight):
    return jnp.einsum('btd,de->bte', values, weight, precision=lax.Precision.HIGHEST)

def gelu_exact(values):
    return jax.nn.gelu(values, approximate=False)

def forward_layer(frozen, values, trainables, allowed):
    w_query, w_key, w_value, w_out, w_up, w_down = frozen
    a_query, b_query, a_value, b_value, gain_one, shift_one, gain_two, shift_two = trainables
    group_size, span_length, model_width = values.shape
    head_shape = (group_size, span_length, H, DH)
    scale_factor = 1.0 / math.sqrt(DH)
    query_low = low_back(low(project(values, a_query)))
    value_low = low_back(low(project(values, a_value)))
    queries = low_back(low(project(values, w_query) + 2.0 * project(query_low, b_query)))
    key_rows = low_back(low(project(values, w_key)))
    value_rows = low_back(low(project(values, w_value) + 2.0 * project(value_low, b_value)))
    raw_scores = jnp.einsum('bqhd,bkhd->bhqk', queries.reshape(head_shape), key_rows.reshape(head_shape), precision=lax.Precision.HIGHEST)
    scores = low_back(raw_scores * scale_factor)
    scores = jnp.where(allowed[:, None, :, :], scores, -1e+30)
    weights = jax.nn.softmax(scores, axis=-1)
    context = jnp.einsum('bhqk,bkhd->bqhd', low(weights), value_rows.reshape(head_shape), precision=lax.Precision.HIGHEST)
    context = low_back(low(context.reshape(group_size, span_length, model_width)))
    attended = low_back(project(context, w_out))
    hidden_one = norm_rows(values + attended, gain_one, shift_one)
    upward = low_back(project(low(hidden_one), w_up))
    active = low(gelu_exact(upward))
    downward = low_back(project(active, w_down))
    return norm_rows(hidden_one + downward, gain_two, shift_two)

def reference(inputs, pair_lengths, w_query, w_key, w_value, w_out, w_up, w_down, a_query, b_query, a_value, b_value, gain_one, shift_one, gain_two, shift_two, cotangent):
    group_size = math.gcd(SEQUENCES, 4)
    group_count = SEQUENCES // group_size
    frozen = tuple((weight.astype(jnp.float32) for weight in (w_query, w_key, w_value, w_out, w_up, w_down)))
    trainable = tuple((weight.astype(jnp.float32) for weight in (a_query, b_query, a_value, b_value, gain_one, shift_one, gain_two, shift_two)))
    blocks = (inputs.reshape(group_count, group_size, LEN, D), pair_lengths.reshape(group_count, group_size, PAIRS), cotangent.reshape(group_count, group_size, LEN, D))

    def scan_step(totals, scan_item):
        block_inputs, block_lengths, block_cotangent = scan_item
        segments = segment_ids(block_lengths, LEN)
        allowed = segments[:, :, None] == segments[:, None, :]

        def layer_of(values, trainables):
            return forward_layer(frozen, values, trainables, allowed)
        outputs, pullback = jax.vjp(layer_of, block_inputs.astype(jnp.float32), trainable)
        grad_values, grad_trainables = pullback(block_cotangent.astype(jnp.float32))
        totals = tuple((running + fresh for running, fresh in zip(totals, grad_trainables)))
        return (totals, (outputs.astype(jnp.bfloat16), grad_values))
    initial = tuple((jnp.zeros(weight.shape, jnp.float32) for weight in trainable))
    totals, (outputs, grad_values) = lax.scan(scan_step, initial, blocks)
    grad_a_query, grad_b_query, grad_a_value, grad_b_value, grad_gain_one, grad_shift_one, grad_gain_two, grad_shift_two = totals
    return (outputs.reshape(SEQUENCES, LEN, D), grad_values.reshape(SEQUENCES, LEN, D), grad_a_query, grad_b_query, grad_a_value, grad_b_value, grad_gain_one, grad_shift_one, grad_gain_two, grad_shift_two)
```

```python
import math

import jax
import jax.numpy as jnp
from jax import lax
from jax.sharding import PartitionSpec as P

DH = 64


norm_epsilon = 1e-05


def matmul(former, latter):
    return jnp.dot(former, latter, preferred_element_type=jnp.float32)


def row_inner(former, latter):
    return lax.dot_general(
        former, latter, (((0,), (0,)), ((), ())), preferred_element_type=jnp.float32
    )


def segment_ids(lengths, span_length):
    pair_ends = jnp.cumsum(lengths, axis=-1)
    places = jnp.arange(span_length, dtype=jnp.int32)
    return jnp.sum((places[None, :, None] >= pair_ends[:, None, :]).astype(jnp.int32), axis=-1)


def norm_rows(values, gain_vec, shift_vec):
    centred = values - jnp.mean(values, axis=-1, keepdims=True)
    variance = jnp.mean(centred * centred, axis=-1, keepdims=True)
    return centred * lax.rsqrt(variance + norm_epsilon) * gain_vec + shift_vec


def gelu_exact(values):
    return jax.nn.gelu(values, approximate=False)


def swap_and_add(values, axis, partners):
    size = lax.axis_size(axis)
    sent = values.astype(jnp.bfloat16)
    arrived = [
        lax.ppermute(sent, axis, [(i, i ^ p) for i in range(size)]) for p in partners
    ]
    for one in arrived:
        values = values + one.astype(jnp.float32)
    return values


def sum_everywhere(values):
    values = swap_and_add(values, "seq", (1,))
    stride, size = 1, lax.axis_size("dp")
    while stride < size:
        radix = min(4, size // stride)
        values = swap_and_add(values, "dp", [stride * k for k in range(1, radix)])
        stride *= radix
    return values


def body(
    inputs,
    pair_lengths,
    w_query,
    w_key,
    w_value,
    w_out,
    w_up,
    w_down,
    a_query,
    b_query,
    a_value,
    b_value,
    gain_one,
    shift_one,
    gain_two,
    shift_two,
    cotangent,
):
    seq_count, half_len, model_width = inputs.shape
    group_size = lax.axis_size("seq")
    span_length = half_len * group_size
    head_count = model_width // DH
    scale_factor = 1.0 / math.sqrt(DH)
    row_count = seq_count * half_len
    own_start = lax.axis_index("seq") * half_len
    flat_inputs = inputs.reshape(row_count, model_width)
    query_low = matmul(flat_inputs, a_query).astype(jnp.bfloat16)
    queries = (matmul(flat_inputs, w_query) + 2.0 * matmul(query_low, b_query)).astype(jnp.bfloat16)
    value_low = matmul(flat_inputs, a_value).astype(jnp.bfloat16)
    key_rows = matmul(flat_inputs, w_key).astype(jnp.bfloat16)
    value_rows = (matmul(flat_inputs, w_value) + 2.0 * matmul(value_low, b_value)).astype(
        jnp.bfloat16
    )
    key_all, value_all = (
        lax.all_gather(
            key_rows.reshape(seq_count, half_len, model_width), "seq", axis=1, tiled=True
        ),
        lax.all_gather(
            value_rows.reshape(seq_count, half_len, model_width), "seq", axis=1, tiled=True
        ),
    )
    segments = segment_ids(pair_lengths, span_length)
    own_segments = lax.dynamic_slice_in_dim(segments, own_start, half_len, 1)
    allowed = own_segments[:, :, None] == segments[:, None, :]
    query_heads = queries.reshape(seq_count, half_len, head_count, DH)
    key_heads = key_all.reshape(seq_count, span_length, head_count, DH)
    value_heads = value_all.reshape(seq_count, span_length, head_count, DH)

    def masked_scores():
        raw_scores = jnp.einsum(
            "sqhd,skhd->shqk", query_heads, key_heads, preferred_element_type=jnp.float32
        )
        return jnp.where(allowed[:, None, :, :], raw_scores * scale_factor, -1e30)

    scores = masked_scores()
    row_peak = jnp.max(scores, axis=-1, keepdims=True)
    raised = jnp.exp(scores - row_peak)
    row_total = jnp.sum(raised, axis=-1, keepdims=True)
    weights = raised / row_total
    log_total = row_peak + jnp.log(row_total)
    context = jnp.einsum(
        "shqk,skhd->sqhd",
        weights.astype(jnp.bfloat16),
        value_heads,
        preferred_element_type=jnp.float32,
    )
    context = context.reshape(row_count, model_width).astype(jnp.bfloat16)
    resid_one = flat_inputs.astype(jnp.float32) + matmul(context, w_out)
    hidden_one, pull_one = jax.vjp(norm_rows, resid_one, gain_one, shift_one)
    upward = matmul(hidden_one.astype(jnp.bfloat16), w_up)
    gelu_values, pull_gelu = jax.vjp(gelu_exact, upward)
    active = gelu_values.astype(jnp.bfloat16)
    resid_two = hidden_one + matmul(active, w_down)
    normed_two, pull_two = jax.vjp(norm_rows, resid_two, gain_two, shift_two)
    grad_out = cotangent.reshape(row_count, model_width).astype(jnp.float32)
    grad_resid_two, grad_gain_two, grad_shift_two = pull_two(grad_out)
    grad_active = matmul(grad_resid_two.astype(jnp.bfloat16), w_down.T)
    grad_up = pull_gelu(grad_active)[0].astype(jnp.bfloat16)
    grad_hidden = grad_resid_two + matmul(grad_up, w_up.T)
    grad_resid_one, grad_gain_one, grad_shift_one = pull_one(grad_hidden)
    grad_context = matmul(grad_resid_one.astype(jnp.bfloat16), w_out.T).astype(jnp.bfloat16)
    grad_context_heads = grad_context.reshape(seq_count, half_len, head_count, DH)
    again = jnp.exp(masked_scores() - log_total)
    grad_weights = jnp.einsum(
        "sqhd,skhd->shqk", grad_context_heads, value_heads, preferred_element_type=jnp.float32
    )
    grad_value_all = jnp.einsum(
        "shqk,sqhd->skhd",
        again.astype(jnp.bfloat16),
        grad_context_heads,
        preferred_element_type=jnp.float32,
    )
    inner_sum = jnp.sum(again * grad_weights, axis=-1, keepdims=True)
    grad_scores = (again * (grad_weights - inner_sum)).astype(jnp.bfloat16)
    grad_query = (
        jnp.einsum("shqk,skhd->sqhd", grad_scores, key_heads, preferred_element_type=jnp.float32)
        * scale_factor
    )
    grad_key_all = (
        jnp.einsum("shqk,sqhd->skhd", grad_scores, query_heads, preferred_element_type=jnp.float32)
        * scale_factor
    )
    returned_key, returned_value = (
        lax.psum_scatter(
            grad_key_all.reshape(seq_count, span_length, model_width),
            "seq",
            scatter_dimension=1,
            tiled=True,
        ),
        lax.psum_scatter(
            grad_value_all.reshape(seq_count, span_length, model_width),
            "seq",
            scatter_dimension=1,
            tiled=True,
        ),
    )
    grad_key = returned_key.reshape(row_count, model_width).astype(jnp.bfloat16)
    grad_value = returned_value.reshape(row_count, model_width).astype(jnp.bfloat16)
    grad_query_low = grad_query.reshape(row_count, model_width).astype(jnp.bfloat16)
    grad_qa = (2.0 * matmul(grad_query_low, b_query.T)).astype(jnp.bfloat16)
    grad_va = (2.0 * matmul(grad_value, b_value.T)).astype(jnp.bfloat16)
    grad_inputs = (
        grad_resid_one
        + matmul(grad_query_low, w_query.T)
        + matmul(grad_key, w_key.T)
        + matmul(grad_value, w_value.T)
        + matmul(grad_qa, a_query.T)
        + matmul(grad_va, a_value.T)
    )
    grad_a_query = row_inner(flat_inputs, grad_qa)
    grad_b_query = 2.0 * row_inner(query_low, grad_query_low)
    grad_a_value = row_inner(flat_inputs, grad_va)
    grad_b_value = 2.0 * row_inner(value_low, grad_value)
    packed = jnp.concatenate(
        [
            grad_a_query.T,
            grad_b_query,
            grad_a_value.T,
            grad_b_value,
            grad_gain_one[None],
            grad_shift_one[None],
            grad_gain_two[None],
            grad_shift_two[None],
        ]
    )
    total = sum_everywhere(packed)
    rank = a_query.shape[1]
    low, high = total[: 2 * rank], total[2 * rank : 4 * rank]
    summed = (low[:rank].T, low[rank:], high[:rank].T, high[rank:]) + tuple(
        total[4 * rank + i] for i in range(4)
    )
    output = normed_two.astype(jnp.bfloat16).reshape(seq_count, half_len, model_width)
    return (
        output,
        grad_inputs.reshape(seq_count, half_len, model_width),
        summed[0],
        summed[1],
        summed[2],
        summed[3],
        summed[4],
        summed[5],
        summed[6],
        summed[7],
    )


def solution(mesh):
    in_specs = (
        P("dp", "seq", None),
        P("dp", None),
        P(),
        P(),
        P(),
        P(),
        P(),
        P(),
        P(),
        P(),
        P(),
        P(),
        P(),
        P(),
        P(),
        P(),
        P("dp", "seq", None),
    )
    out_specs = (P("dp", "seq", None), P("dp", "seq", None), P(), P(), P(), P(), P(), P(), P(), P())
    return jax.shard_map(body, mesh=mesh, in_specs=in_specs, out_specs=out_specs, check_vma=False)
```

```python
import functools
import math

import jax
import jax.numpy as jnp
from jax import lax
from jax.experimental import pallas as pl
from jax.experimental.pallas import tpu as pltpu
from jax.sharding import PartitionSpec as P

DH = 64
LANES = 128
EPSILON = 1e-05
LOG2_E = math.log2(math.e)
FAR_AWAY = -1e30
BF16 = jnp.bfloat16
F32 = jnp.float32
NN = ((1,), (0,))
NT = ((1,), (1,))
TN = ((0,), (0,))
TT = ((0,), (1,))


def dot(former, latter, dims=NN):
    return lax.dot_general(former, latter, (dims, ((), ())), preferred_element_type=F32)


def normed(values):
    centred = values - jnp.mean(values, axis=-1, keepdims=True)
    variance = jnp.mean(centred * centred, axis=-1, keepdims=True)
    inverse = lax.rsqrt(variance + EPSILON)
    return centred * inverse, inverse


def norm_back(grad, normal, inverse):
    return inverse * (
        grad
        - jnp.mean(grad, axis=-1, keepdims=True)
        - normal * jnp.mean(grad * normal, axis=-1, keepdims=True)
    )


def gelu_and_slope(values):
    size = jnp.abs(values)
    inv = 1.0 / (1.0 + (0.3275911 / math.sqrt(2.0)) * size)
    bell = jnp.exp2(values * values * (-0.5 * LOG2_E))
    tail = inv * (
        0.5 * 0.254829592
        + inv
        * (
            0.5 * -0.284496736
            + inv * (0.5 * 1.421413741 + inv * (0.5 * -1.453152027 + inv * (0.5 * 1.061405429)))
        )
    )
    tail = tail * bell
    below = jnp.where(values < 0.0, tail, 1.0 - tail)
    return values * below, below + values * bell * (1.0 / math.sqrt(2.0 * math.pi))


def segment_codes(lengths_ref, start_near, start_far, rows):
    row = lax.broadcasted_iota(jnp.int32, (rows, LANES), 0)
    half = rows // 2
    place = jnp.where(row < half, start_near + row, start_far + row - half)
    segment = jnp.zeros_like(place)
    end = jnp.int32(0)
    for pair in range(lengths_ref.shape[1]):
        end = end + lengths_ref[0, pair]
        segment = segment + (place >= end).astype(jnp.int32)
    return segment


def crosses_widely(lengths_ref, middle, half):
    end = jnp.int32(0)
    left = jnp.int32(middle)
    right = jnp.int32(middle)
    for pair in range(lengths_ref.shape[1]):
        end = end + lengths_ref[0, pair]
        left = jnp.where(end < middle, middle - end, left)
        right = jnp.where(end >= middle, jnp.minimum(right, end - middle), right)
    return (right > 0) & ((left > half) | (right > half))


def layer_kernel(
    lengths_ref,
    x_hbm,
    other_hbm,
    wq_hbm,
    wk_hbm,
    wv_hbm,
    wo_hbm,
    wu_hbm,
    wd_hbm,
    small_hbm,
    gains_hbm,
    cot_hbm,
    out_hbm,
    gr_hbm,
    dqt_hbm,
    dk_hbm,
    dv_hbm,
    packed_ref,
    x_s,
    wq,
    wk,
    wv,
    wo,
    wu,
    wd,
    small,
    gains,
    cot_s,
    q_s,
    k_s,
    v_s,
    kt_s,
    vt_s,
    po_s,
    ph_s,
    inv_s,
    ct_s,
    normal_s,
    rstd_s,
    hidden_s,
    active_s,
    slope_s,
    total_s,
    out_s,
    gr_s,
    dot_s,
    dqt_s,
    dk_s,
    dv_s,
    sems,
):
    tokens, width = x_hbm.shape[1:]
    half = tokens // 2
    hidden = wu_hbm.shape[1]
    rank = small_hbm.shape[0] // 4
    heads = width // DH
    side = lax.axis_index("seq")
    near = pl.multiple_of((1 - side) * half, half)
    far = pl.multiple_of(side * half, half)

    copies = []

    def fetch(source, target):
        copy = pltpu.make_async_copy(source, target, sems.at[len(copies)])
        copies.append(copy)
        copy.start()
        return copy

    get_x = [
        fetch(x_hbm.at[0, pl.ds(near, half)], x_s.at[pl.ds(0, half)]),
        fetch(x_hbm.at[0, pl.ds(far, half)], x_s.at[pl.ds(half, half)]),
        fetch(other_hbm.at[0, pl.ds(far, half)], x_s.at[pl.ds(tokens, half)]),
        fetch(other_hbm.at[0, pl.ds(near, half)], x_s.at[pl.ds(tokens + half, half)]),
        fetch(small_hbm, small),
    ]
    get_q = fetch(wq_hbm, wq)
    get_k = fetch(wk_hbm, wk)
    get_v = fetch(wv_hbm, wv)
    get_o = fetch(wo_hbm, wo)
    get_gains = fetch(gains_hbm, gains)
    chunks = hidden // width
    get_u, get_d = [], []
    for c in range(chunks):
        get_u.append(
            fetch(wu_hbm.at[:, pl.ds(c * width, width)], wu.at[:, pl.ds(c * width, width)])
        )
        get_d.append(fetch(wd_hbm.at[pl.ds(c * width, width)], wd.at[pl.ds(c * width, width)]))
    get_cot = [
        fetch(cot_hbm.at[0, pl.ds(near, half)], cot_s.at[pl.ds(0, half)]),
        fetch(cot_hbm.at[0, pl.ds(far, half)], cot_s.at[pl.ds(half, half)]),
    ]

    wide = crosses_widely(lengths_ref, tokens, half)
    own_segment = segment_codes(lengths_ref, side * tokens + near, side * tokens + far, tokens)
    halo_base = (1 - side) * tokens
    halo_segment = segment_codes(lengths_ref, halo_base + far, halo_base + near, tokens)
    lane = lax.broadcasted_iota(jnp.int32, (tokens, LANES), 1)
    code = lane & (DH - 1)
    low_half = lane < DH
    marks = lengths_ref.shape[1] + 1
    q_code = jnp.where(code == own_segment, 1.0, 0.0).astype(BF16)

    def key_code(segment):
        return jnp.where((code < marks) & (code != segment), FAR_AWAY, 0.0).astype(BF16)

    ko_code = key_code(own_segment)
    kh_code = key_code(halo_segment)

    for copy in get_x:
        copy.wait()
    narrow = tokens + half
    aqt, bq = small[pl.ds(0, rank)], small[pl.ds(rank, rank)]
    avt, bv = small[pl.ds(2 * rank, rank)], small[pl.ds(3 * rank, rank)]
    x_all = x_s[pl.ds(0, narrow)]
    x_own = x_s[pl.ds(0, tokens)]
    qlow_t = dot(aqt, x_own, NT).astype(BF16)
    vlow_t = dot(avt, x_s[...], NT).astype(BF16)
    get_q.wait()
    q_s[...] = (
        (dot(x_own, wq[...]) + 2.0 * dot(qlow_t, bq, TN)) * (LOG2_E / math.sqrt(DH))
    ).astype(BF16)
    get_k.wait()
    keys = dot(x_all, wk[...]).astype(BF16)
    k_s[pl.ds(0, narrow)] = keys
    kt_s[:, pl.ds(0, narrow)] = keys.T
    get_v.wait()
    vals = (dot(x_all, wv[...]) + 2.0 * dot(vlow_t[:, :narrow], bv, TN)).astype(BF16)
    v_s[pl.ds(0, narrow)] = vals
    vt_s[:, pl.ds(0, narrow)] = vals.T

    @pl.when(wide)
    def _():
        x_far = x_s[pl.ds(narrow, half)]
        keys = dot(x_far, wk[...]).astype(BF16)
        k_s[pl.ds(narrow, half)] = keys
        kt_s[:, pl.ds(narrow, half)] = keys.T
        vals = (dot(x_far, wv[...]) + 2.0 * dot(vlow_t[:, narrow:], bv, TN)).astype(BF16)
        v_s[pl.ds(narrow, half)] = vals
        vt_s[:, pl.ds(narrow, half)] = vals.T

    def joined(own, halo, reach, join):
        if reach == tokens:
            return join(own, halo)
        return jnp.concatenate([join(own[:, :reach], halo), own[:, reach:]], axis=1)

    def attend(pair, reach):
        lanes = pl.ds(pl.multiple_of(pair * LANES, LANES), LANES)
        q_pair = q_s[:, lanes]
        ko_pair = k_s[pl.ds(0, tokens), lanes]
        kh_pair = k_s[pl.ds(tokens, reach), lanes]
        for odd in range(2):
            head = 2 * pair + odd
            rows = pl.ds(pl.multiple_of(head * DH, DH), DH)

            def mixed(values, codes):
                mask = low_half[: values.shape[0]]
                if odd:
                    return jnp.where(mask, codes, values)
                return jnp.where(mask, values, codes)

            q_head = mixed(q_pair, q_code)
            own = dot(mixed(ko_pair, ko_code), q_head, NT)
            halo = dot(mixed(kh_pair, kh_code[:reach]), q_head[:reach], NT)
            peak = joined(
                jnp.max(own, axis=0, keepdims=True),
                jnp.max(halo, axis=0, keepdims=True),
                reach,
                jnp.maximum,
            )
            own = jnp.exp2(own - peak)
            halo = jnp.exp2(halo - peak[:, :reach])
            inverse = 1.0 / joined(
                jnp.sum(own, axis=0, keepdims=True),
                jnp.sum(halo, axis=0, keepdims=True),
                reach,
                jnp.add,
            )
            own, halo = own.astype(BF16), halo.astype(BF16)
            po_s[head] = own
            ph_s[head, pl.ds(0, reach), pl.ds(0, reach)] = halo
            inv_s[head] = jnp.broadcast_to(inverse, inv_s.shape[1:])
            context = joined(
                dot(vt_s[rows, pl.ds(0, tokens)], own),
                dot(vt_s[rows, pl.ds(tokens, reach)], halo),
                reach,
                jnp.add,
            )
            ct_s[rows, :] = (context * inverse).astype(BF16)

    def attend_back(pair, reach):
        lanes = pl.ds(pl.multiple_of(pair * LANES, LANES), LANES)
        q_pair = q_s[:, lanes]
        vo_pair = v_s[pl.ds(0, tokens), lanes]
        vh_pair = v_s[pl.ds(tokens, reach), lanes]
        dv_own, dv_halo, dk_own, dk_halo = [], [], [], []
        for odd in range(2):
            head = 2 * pair + odd
            rows = pl.ds(pl.multiple_of(head * DH, DH), DH)
            inverse = inv_s[head, pl.ds(0, 1), :]
            grad = (dot_s[rows, :] * inverse).astype(BF16)
            blank = jnp.zeros_like(grad)
            grad = jnp.concatenate([blank, grad] if odd else [grad, blank], axis=0)
            po, ph = po_s[head], ph_s[head, pl.ds(0, reach), pl.ds(0, reach)]
            own = po.astype(F32) * dot(vo_pair, grad)
            halo = ph.astype(F32) * dot(vh_pair, grad[:, :reach])
            inner = inverse * joined(
                jnp.sum(own, axis=0, keepdims=True),
                jnp.sum(halo, axis=0, keepdims=True),
                reach,
                jnp.add,
            )
            own = (own - po.astype(F32) * inner).astype(BF16)
            halo = (halo - ph.astype(F32) * inner[:, :reach]).astype(BF16)
            dv_own.append(dot(po, grad, NT))
            dv_halo.append(dot(ph, grad[:, :reach], NT))
            dk_own.append(dot(own, q_pair))
            dk_halo.append(dot(halo, q_pair[:reach]))
            dqt = joined(
                dot(kt_s[rows, pl.ds(0, tokens)], own),
                dot(kt_s[rows, pl.ds(tokens, reach)], halo),
                reach,
                jnp.add,
            )
            dqt_s[rows, :] = (dqt * (1.0 / math.sqrt(DH))).astype(BF16)
        unscale = 1.0 / LOG2_E
        dv_s[pl.ds(0, tokens), lanes] = (dv_own[0] + dv_own[1]).astype(BF16)
        dv_s[pl.ds(tokens, reach), lanes] = (dv_halo[0] + dv_halo[1]).astype(BF16)
        dk_s[pl.ds(0, tokens), lanes] = (
            jnp.where(low_half, dk_own[0], dk_own[1]) * unscale
        ).astype(BF16)
        dk_s[pl.ds(tokens, reach), lanes] = (
            jnp.where(low_half[:reach], dk_halo[0], dk_halo[1]) * unscale
        ).astype(BF16)

    def for_pairs(step):
        @pl.when(jnp.logical_not(wide))
        def _():
            for pair in range(heads // 2):
                step(pair, half)

        @pl.when(wide)
        def _():
            lax.fori_loop(0, heads // 2, lambda pair, none: step(pair, tokens), None)

    for_pairs(attend)

    get_o.wait()
    get_gains.wait()
    resid_one = x_own.astype(F32) + dot(ct_s[...], wo[...], TN)
    normal, inverse = normed(resid_one)
    normal_s[...] = normal
    rstd_s[...] = jnp.broadcast_to(inverse, rstd_s.shape)
    gain_one, shift_one = gains[pl.ds(0, 1), :], gains[pl.ds(1, 1), :]
    gain_two, shift_two = gains[pl.ds(2, 1), :], gains[pl.ds(3, 1), :]
    hidden_one = normal * gain_one + shift_one
    hidden_s[...] = hidden_one.astype(BF16)
    total_s[...] = hidden_one
    for c in range(chunks):
        part = pl.ds(c * width, width)
        get_u[c].wait()
        upward = dot(hidden_s[...], wu[:, part])
        value, slope = gelu_and_slope(upward)
        active_s[:, part] = value.astype(BF16)
        slope_s[:, part] = slope.astype(BF16)
        get_d[c].wait()
        total_s[...] += dot(active_s[:, part], wd[part, :])
    normal_two, inverse_two = normed(total_s[...])
    out_s[...] = (normal_two * gain_two + shift_two).astype(BF16)

    def put(source, target):
        return fetch(source, target)

    puts = [
        put(out_s.at[pl.ds(0, half)], out_hbm.at[0, pl.ds(near, half)]),
        put(out_s.at[pl.ds(half, half)], out_hbm.at[0, pl.ds(far, half)]),
    ]
    for copy in get_cot:
        copy.wait()
    grad_out = cot_s[...].astype(F32)
    packed_ref[pl.ds(4 * rank + 2, 1), :] = jnp.sum(grad_out * normal_two, axis=0, keepdims=True)
    packed_ref[pl.ds(4 * rank + 3, 1), :] = jnp.sum(grad_out, axis=0, keepdims=True)
    grad_two = norm_back(grad_out * gain_two, normal_two, inverse_two)
    hidden_s[...] = grad_two.astype(BF16)
    total_s[...] = grad_two
    for c in range(chunks):
        part = pl.ds(c * width, width)
        grad_up = slope_s[:, part].astype(F32) * dot(hidden_s[...], wd[part, :], NT)
        active_s[:, part] = grad_up.astype(BF16)
        total_s[...] += dot(active_s[:, part], wu[:, part], NT)
    grad_hidden = total_s[...]
    normal = normal_s[...]
    packed_ref[pl.ds(4 * rank, 1), :] = jnp.sum(grad_hidden * normal, axis=0, keepdims=True)
    packed_ref[pl.ds(4 * rank + 1, 1), :] = jnp.sum(grad_hidden, axis=0, keepdims=True)
    grad_one = norm_back(grad_hidden * gain_one, normal, rstd_s[:, :1])
    gr_s[...] = grad_one
    puts.append(put(gr_s, gr_hbm))
    dot_s[...] = dot(wo[...], grad_one.astype(BF16), NT)

    @pl.when(jnp.logical_not(wide))
    def _():
        dk_s[pl.ds(narrow, half)] = jnp.zeros((half, width), BF16)
        dv_s[pl.ds(narrow, half)] = jnp.zeros((half, width), BF16)

    for_pairs(attend_back)

    puts.append(put(dqt_s, dqt_hbm))
    puts.append(put(dk_s, dk_hbm))
    puts.append(put(dv_s, dv_hbm))
    grad_qlow_t = (2.0 * dot(bq, dqt_s[...])).astype(BF16)
    packed_ref[pl.ds(0, rank), :] = dot(grad_qlow_t, x_own)
    packed_ref[pl.ds(rank, rank), :] = 2.0 * dot(qlow_t, dqt_s[...], NT)
    grad_vlow_t = (2.0 * dot(bv, dv_s[...], NT)).astype(BF16)
    packed_ref[pl.ds(2 * rank, rank), :] = dot(grad_vlow_t, x_s[...])
    packed_ref[pl.ds(3 * rank, rank), :] = 2.0 * dot(vlow_t, dv_s[...])
    spare = packed_ref.shape[0] - 4 * rank - 4
    packed_ref[pl.ds(4 * rank + 4, spare), :] = jnp.zeros((spare, width), F32)
    for copy in puts:
        copy.wait()


def call_layer(lengths, x, other, weights, small, gains, cotangent):
    wq, wk, wv, wo, wu, wd = weights
    _, tokens, width = x.shape
    hidden = wu.shape[1]
    heads = width // DH
    rank = small.shape[0] // 4
    packed_rows = -(-(4 * rank + 4) // 16) * 16
    hbm = pl.BlockSpec(memory_space=pltpu.HBM)
    shape = jax.ShapeDtypeStruct
    vmem = pltpu.VMEM
    return pl.pallas_call(
        layer_kernel,
        out_shape=(
            shape((1, tokens, width), BF16),
            shape((tokens, width), F32),
            shape((width, tokens), BF16),
            shape((2 * tokens, width), BF16),
            shape((2 * tokens, width), BF16),
            shape((packed_rows, width), F32),
        ),
        in_specs=[pl.BlockSpec(memory_space=pltpu.SMEM)] + [hbm] * 11,
        out_specs=(hbm,) * 5 + (pl.BlockSpec(memory_space=pltpu.VMEM),),
        scratch_shapes=[
            vmem((2 * tokens, width), BF16),
            vmem(wq.shape, BF16),
            vmem(wk.shape, BF16),
            vmem(wv.shape, BF16),
            vmem(wo.shape, BF16),
            vmem(wu.shape, BF16),
            vmem(wd.shape, BF16),
            vmem(small.shape, BF16),
            vmem(gains.shape, F32),
            vmem((tokens, width), BF16),
            vmem((tokens, width), BF16),
            vmem((2 * tokens, width), BF16),
            vmem((2 * tokens, width), BF16),
            vmem((width, 2 * tokens), BF16),
            vmem((width, 2 * tokens), BF16),
            vmem((heads, tokens, tokens), BF16),
            vmem((heads, tokens, tokens), BF16),
            vmem((heads, 8, tokens), F32),
            vmem((width, tokens), BF16),
            vmem((tokens, width), F32),
            vmem((tokens, LANES), F32),
            vmem((tokens, width), BF16),
            vmem((tokens, hidden), BF16),
            vmem((tokens, hidden), BF16),
            vmem((tokens, width), F32),
            vmem((tokens, width), BF16),
            vmem((tokens, width), F32),
            vmem((width, tokens), F32),
            vmem((width, tokens), BF16),
            vmem((2 * tokens, width), BF16),
            vmem((2 * tokens, width), BF16),
            pltpu.SemaphoreType.DMA((32,)),
        ],
        compiler_params=pltpu.CompilerParams(vmem_limit_bytes=60 * 2**20),
    )(lengths, x, other, wq, wk, wv, wo, wu, wd, small, gains, cotangent)


def inputs_kernel(
    gr_ref, dqt_ref, dk_ref, dv_ref, hk_ref, hv_ref, wq, wk, wv, small, out_hbm, out_s, sems
):
    tokens, width = gr_ref.shape
    half = tokens // 2
    rank = small.shape[0] // 4
    side = lax.axis_index("seq")
    near = pl.multiple_of((1 - side) * half, half)
    far = pl.multiple_of(side * half, half)
    aqt, bq = small[pl.ds(0, rank)], small[pl.ds(rank, rank)]
    avt, bv = small[pl.ds(2 * rank, rank)], small[pl.ds(3 * rank, rank)]
    dqt = dqt_ref[...]
    dk = (dk_ref[...].astype(F32) + hk_ref[...].astype(F32)).astype(BF16)
    dv = (dv_ref[...].astype(F32) + hv_ref[...].astype(F32)).astype(BF16)
    grad_qlow_t = (2.0 * dot(bq, dqt)).astype(BF16)
    grad_vlow_t = (2.0 * dot(bv, dv, NT)).astype(BF16)
    out_s[...] = (
        gr_ref[...]
        + dot(dqt, wq[...], TT)
        + dot(dk, wk[...], NT)
        + dot(dv, wv[...], NT)
        + dot(grad_qlow_t, aqt, TN)
        + dot(grad_vlow_t, avt, TN)
    )
    puts = [
        pltpu.make_async_copy(
            out_s.at[pl.ds(0, half)], out_hbm.at[0, pl.ds(near, half)], sems.at[0]
        ),
        pltpu.make_async_copy(
            out_s.at[pl.ds(half, half)], out_hbm.at[0, pl.ds(far, half)], sems.at[1]
        ),
    ]
    for copy in puts:
        copy.start()
    for copy in puts:
        copy.wait()


def call_inputs(gr, dqt, dk, dv, hk, hv, wq, wk, wv, small):
    tokens, width = gr.shape

    def top(rows):
        return pl.BlockSpec((rows, width), lambda i: (0, 0))

    whole = pl.BlockSpec((width, width), lambda i: (0, 0))
    return pl.pallas_call(
        inputs_kernel,
        grid=(1,),
        out_shape=jax.ShapeDtypeStruct((1, tokens, width), F32),
        in_specs=[
            top(tokens),
            pl.BlockSpec((width, tokens), lambda i: (0, 0)),
            top(tokens),
            top(tokens),
            top(tokens),
            top(tokens),
            whole,
            whole,
            whole,
            top(small.shape[0]),
        ],
        out_specs=pl.BlockSpec(memory_space=pltpu.HBM),
        scratch_shapes=[pltpu.VMEM((tokens, width), F32), pltpu.SemaphoreType.DMA((2,))],
        compiler_params=pltpu.CompilerParams(vmem_limit_bytes=60 * 2**20),
    )(gr, dqt, dk, dv, hk, hv, wq, wk, wv, small)


def swap_and_add(values, axis, partners):
    size = lax.axis_size(axis)
    arrived = [
        lax.ppermute(values, axis, [(i, i ^ p) for i in range(size)]) for p in partners
    ]
    total = values.astype(F32)
    for one in arrived:
        total = total + one.astype(F32)
    return total


def sum_everywhere(values):
    values = swap_and_add(values.astype(BF16), "seq", (1,))
    stride, size = 1, lax.axis_size("dp")
    while stride < size:
        radix = min(4, size // stride)
        values = swap_and_add(
            values.astype(BF16), "dp", [stride * k for k in range(1, radix)]
        )
        stride *= radix
    return values


def body(
    inputs,
    pair_lengths,
    w_query,
    w_key,
    w_value,
    w_out,
    w_up,
    w_down,
    a_query,
    b_query,
    a_value,
    b_value,
    gain_one,
    shift_one,
    gain_two,
    shift_two,
    cotangent,
):
    tokens = inputs.shape[1]
    rank = a_query.shape[1]
    swap = [(0, 1), (1, 0)]
    other = lax.ppermute(inputs, "seq", swap)
    small = jnp.concatenate([a_query.T, b_query, a_value.T, b_value])
    gains = jnp.stack([gain_one, shift_one, gain_two, shift_two])
    output, gr, dqt, dk, dv, packed = call_layer(
        pair_lengths,
        inputs,
        other,
        (w_query, w_key, w_value, w_out, w_up, w_down),
        small,
        gains,
        cotangent,
    )
    total = sum_everywhere(packed)
    hk = lax.ppermute(dk[tokens:], "seq", swap)
    hv = lax.ppermute(dv[tokens:], "seq", swap)
    grad_inputs = call_inputs(gr, dqt, dk, dv, hk, hv, w_query, w_key, w_value, small)
    return (
        output,
        grad_inputs,
        total[:rank].T,
        total[rank : 2 * rank],
        total[2 * rank : 3 * rank].T,
        total[3 * rank : 4 * rank],
        total[4 * rank],
        total[4 * rank + 1],
        total[4 * rank + 2],
        total[4 * rank + 3],
    )


def solution(mesh):
    tokens = P("dp", "seq", None)
    in_specs = (tokens, P("dp", None)) + (P(),) * 14 + (tokens,)
    out_specs = (tokens, tokens) + (P(),) * 8
    return jax.shard_map(body, mesh=mesh, in_specs=in_specs, out_specs=out_specs, check_vma=False)
```

```python
import functools
import math

import jax
import jax.numpy as jnp
from jax import lax
from jax.experimental import pallas as pl
from jax.experimental.pallas import tpu as pltpu
from jax.sharding import PartitionSpec as P

DH = 64
LANES = 128
EPSILON = 1e-05
LOG2_E = math.log2(math.e)
FAR_AWAY = -1e30
BF16 = jnp.bfloat16
F32 = jnp.float32
NN = ((1,), (0,))
NT = ((1,), (1,))
TN = ((0,), (0,))
TT = ((0,), (1,))


def dot(former, latter, dims=NN):
    return lax.dot_general(former, latter, (dims, ((), ())), preferred_element_type=F32)


def normed(values):
    centred = values - jnp.mean(values, axis=-1, keepdims=True)
    variance = jnp.mean(centred * centred, axis=-1, keepdims=True)
    inverse = lax.rsqrt(variance + EPSILON)
    return centred * inverse, inverse


def norm_back(grad, normal, inverse):
    return inverse * (
        grad
        - jnp.mean(grad, axis=-1, keepdims=True)
        - normal * jnp.mean(grad * normal, axis=-1, keepdims=True)
    )


def gelu_and_slope(values):
    size = jnp.abs(values)
    inv = 1.0 / (1.0 + (0.3275911 / math.sqrt(2.0)) * size)
    bell = jnp.exp2(values * values * (-0.5 * LOG2_E))
    tail = inv * (
        0.5 * 0.254829592
        + inv
        * (
            0.5 * -0.284496736
            + inv * (0.5 * 1.421413741 + inv * (0.5 * -1.453152027 + inv * (0.5 * 1.061405429)))
        )
    )
    tail = tail * bell
    below = jnp.where(values < 0.0, tail, 1.0 - tail)
    return values * below, below + values * bell * (1.0 / math.sqrt(2.0 * math.pi))


def segment_codes(lengths_ref, start_near, start_far, rows):
    row = lax.broadcasted_iota(jnp.int32, (rows, LANES), 0)
    half = rows // 2
    place = jnp.where(row < half, start_near + row, start_far + row - half)
    segment = jnp.zeros_like(place)
    end = jnp.int32(0)
    for pair in range(lengths_ref.shape[1]):
        end = end + lengths_ref[0, pair]
        segment = segment + (place >= end).astype(jnp.int32)
    return segment


def crosses_widely(lengths_ref, middle, half):
    end = jnp.int32(0)
    left = jnp.int32(middle)
    right = jnp.int32(middle)
    for pair in range(lengths_ref.shape[1]):
        end = end + lengths_ref[0, pair]
        left = jnp.where(end < middle, middle - end, left)
        right = jnp.where(end >= middle, jnp.minimum(right, end - middle), right)
    return (right > 0) & ((left > half) | (right > half))


def in_hbm(*arrays):
    return [pltpu.with_memory_space_constraint(a, pltpu.HBM) for a in arrays]


def own_rows(side, half):
    return pl.multiple_of((1 - side) * half, half), pl.multiple_of(side * half, half)


def project_kernel(
    x_hbm,
    wq_hbm,
    wk_hbm,
    wv_hbm,
    aqt_hbm,
    bq_hbm,
    avt_hbm,
    bv_hbm,
    x_ref,
    q_ref,
    k_ref,
    v_ref,
    kt_ref,
    vt_ref,
    qlow_ref,
    vlow_ref,
    wk,
    wv,
    bq,
    avt,
    bv,
    wq,
    aqt,
    sems,
):
    tokens = x_hbm.shape[1]
    half = tokens // 2
    near, far = own_rows(lax.axis_index("seq"), half)
    pairs = (
        (x_hbm.at[0, pl.ds(near, half)], x_ref.at[pl.ds(0, half)]),
        (x_hbm.at[0, pl.ds(far, half)], x_ref.at[pl.ds(half, half)]),
        (wk_hbm, wk),
        (aqt_hbm, aqt),
        (bq_hbm, bq),
        (avt_hbm, avt),
        (bv_hbm, bv),
        (wq_hbm, wq),
        (wv_hbm, wv),
    )
    copies = [pltpu.make_async_copy(a, b, sems.at[i]) for i, (a, b) in enumerate(pairs)]
    for copy in copies:
        copy.start()
    for copy in copies[:3]:
        copy.wait()
    x = x_ref[...]
    keys = dot(x, wk[...]).astype(BF16)
    k_ref[...] = keys
    kt_ref[...] = keys.T
    for copy in copies[3:]:
        copy.wait()
    qlow_t = dot(aqt[...], x, NT).astype(BF16)
    vlow_t = dot(avt[...], x, NT).astype(BF16)
    qlow_ref[...] = qlow_t
    vlow_ref[...] = vlow_t
    q_ref[...] = (
        (dot(x, wq[...]) + 2.0 * dot(qlow_t, bq[...], TN)) * (LOG2_E / math.sqrt(DH))
    ).astype(BF16)
    vals = (dot(x, wv[...]) + 2.0 * dot(vlow_t, bv[...], TN)).astype(BF16)
    v_ref[...] = vals
    vt_ref[...] = vals.T


def call_project(x, wq, wk, wv, lows):
    _, tokens, width = x.shape
    rank = lows[1].shape[0]
    shape = jax.ShapeDtypeStruct
    rows, columns = shape((tokens, width), BF16), shape((width, tokens), BF16)
    low = shape((rank, tokens), BF16)
    square, flat = shape((width, width), BF16), shape((rank, width), BF16)
    return pl.pallas_call(
        project_kernel,
        out_shape=(rows,) * 4 + (columns,) * 2 + (low,) * 2 + (square,) * 2 + (flat,) * 3,
        in_specs=[pl.BlockSpec(memory_space=pltpu.HBM)] * 8,
        out_specs=(pl.BlockSpec(memory_space=pltpu.VMEM),) * 13,
        scratch_shapes=[
            pltpu.VMEM((width, width), BF16),
            pltpu.VMEM((rank, width), BF16),
            pltpu.SemaphoreType.DMA((9,)),
        ],
        compiler_params=pltpu.CompilerParams(vmem_limit_bytes=14 * 2**20),
        cost_estimate=pl.CostEstimate(flops=10**9, bytes_accessed=8 * 10**6, transcendentals=0),
    )(*in_hbm(x, wq, wk, wv, *lows))


def layer_kernel(
    lengths_ref,
    x_ref,
    q_s,
    k_s,
    v_s,
    kt_s,
    vt_s,
    qlow_ref,
    vlow_ref,
    wk,
    wv,
    bq_ref,
    avt_ref,
    bv_ref,
    other_ref,
    gain_one_hbm,
    shift_one_hbm,
    gain_two_hbm,
    shift_two_hbm,
    wo_hbm,
    wu_hbm,
    wd_hbm,
    cot_hbm,
    out_hbm,
    gr_s,
    dqt_s,
    dk_s,
    dv_s,
    halo_s,
    packed_ref,
    gain_one_s,
    shift_one_s,
    gain_two_s,
    shift_two_s,
    x_s,
    wo,
    wu,
    wd,
    cot_s,
    kh_s,
    vh_s,
    kht_s,
    vht_s,
    po_s,
    ph_s,
    inv_s,
    ct_s,
    normal_s,
    rstd_s,
    hidden_s,
    active_s,
    slope_s,
    total_s,
    out_s,
    dot_s,
    sems,
):
    tokens, width = x_ref.shape
    half = tokens // 2
    hidden = wu_hbm.shape[1]
    rank = bq_ref.shape[0]
    heads = width // DH
    side = lax.axis_index("seq")
    near, far = own_rows(side, half)

    copies = []

    def fetch(source, target):
        copy = pltpu.make_async_copy(source, target, sems.at[len(copies)])
        copies.append(copy)
        copy.start()
        return copy

    get_o = [
        fetch(wo_hbm, wo),
        fetch(gain_one_hbm, gain_one_s),
        fetch(shift_one_hbm, shift_one_s),
        fetch(gain_two_hbm, gain_two_s),
        fetch(shift_two_hbm, shift_two_s),
    ]
    chunks = hidden // width
    get_u, get_d = [], []
    for c in range(chunks):
        part = pl.ds(c * width, width)
        get_u.append(fetch(wu_hbm.at[:, part], wu.at[:, part]))
        get_d.append(fetch(wd_hbm.at[part], wd.at[part]))
    get_cot = [
        fetch(cot_hbm.at[0, pl.ds(near, half)], cot_s.at[pl.ds(0, half)]),
        fetch(cot_hbm.at[0, pl.ds(far, half)], cot_s.at[pl.ds(half, half)]),
    ]

    wide = crosses_widely(lengths_ref, tokens, half)
    own_segment = segment_codes(lengths_ref, side * tokens + near, side * tokens + far, tokens)
    halo_base = (1 - side) * tokens
    halo_segment = segment_codes(lengths_ref, halo_base + far, halo_base + near, tokens)
    lane = lax.broadcasted_iota(jnp.int32, (tokens, LANES), 1)
    code = lane & (DH - 1)
    low_half = lane < DH
    marks = lengths_ref.shape[1] + 1
    q_code = jnp.where(code == own_segment, 1.0, 0.0).astype(BF16)

    def key_code(segment):
        return jnp.where((code < marks) & (code != segment), FAR_AWAY, 0.0).astype(BF16)

    ko_code = key_code(own_segment)
    kh_code = key_code(halo_segment)

    bq, avt, bv = bq_ref[...], avt_ref[...], bv_ref[...]
    qlow_t, vlow_t = qlow_ref[...], vlow_ref[...]
    x_s[pl.ds(0, half)] = other_ref[0, pl.ds(far, half)]
    x_s[pl.ds(half, half)] = other_ref[0, pl.ds(near, half)]
    halo_low_t = dot(avt, x_s[...], NT).astype(BF16)

    def project_halo(start):
        rows = pl.ds(start, half)
        x_halo = x_s[rows]
        keys = dot(x_halo, wk[...]).astype(BF16)
        kh_s[rows] = keys
        kht_s[:, rows] = keys.T
        low_t = halo_low_t[:, start : start + half]
        vals = (dot(x_halo, wv[...]) + 2.0 * dot(low_t, bv, TN)).astype(BF16)
        vh_s[rows] = vals
        vht_s[:, rows] = vals.T

    project_halo(0)

    @pl.when(wide)
    def _():
        project_halo(half)

    def joined(own, halo, reach, join):
        if reach == tokens:
            return join(own, halo)
        return jnp.concatenate([join(own[:, :reach], halo), own[:, reach:]], axis=1)

    def attend(pair, reach):
        lanes = pl.ds(pl.multiple_of(pair * LANES, LANES), LANES)
        q_pair = q_s[:, lanes]
        ko_pair = k_s[:, lanes]
        kh_pair = kh_s[pl.ds(0, reach), lanes]
        for odd in range(2):
            head = 2 * pair + odd
            rows = pl.ds(pl.multiple_of(head * DH, DH), DH)

            def mixed(values, codes):
                mask = low_half[: values.shape[0]]
                if odd:
                    return jnp.where(mask, codes, values)
                return jnp.where(mask, values, codes)

            q_head = mixed(q_pair, q_code)
            own = dot(mixed(ko_pair, ko_code), q_head, NT)
            halo = dot(mixed(kh_pair, kh_code[:reach]), q_head[:reach], NT)
            peak = joined(
                jnp.max(own, axis=0, keepdims=True),
                jnp.max(halo, axis=0, keepdims=True),
                reach,
                jnp.maximum,
            )
            own = jnp.exp2(own - peak)
            halo = jnp.exp2(halo - peak[:, :reach])
            inverse = 1.0 / joined(
                jnp.sum(own, axis=0, keepdims=True),
                jnp.sum(halo, axis=0, keepdims=True),
                reach,
                jnp.add,
            )
            own, halo = own.astype(BF16), halo.astype(BF16)
            po_s[head] = own
            ph_s[head, pl.ds(0, reach), pl.ds(0, reach)] = halo
            inv_s[head] = jnp.broadcast_to(inverse, inv_s.shape[1:])
            context = joined(
                dot(vt_s[rows, :], own),
                dot(vht_s[rows, pl.ds(0, reach)], halo),
                reach,
                jnp.add,
            )
            ct_s[rows, :] = (context * inverse).astype(BF16)

    def attend_back(pair, reach):
        lanes = pl.ds(pl.multiple_of(pair * LANES, LANES), LANES)
        q_pair = q_s[:, lanes]
        vo_pair = v_s[:, lanes]
        vh_pair = vh_s[pl.ds(0, reach), lanes]
        dv_own, dv_halo, dk_own, dk_halo = [], [], [], []
        for odd in range(2):
            head = 2 * pair + odd
            rows = pl.ds(pl.multiple_of(head * DH, DH), DH)
            inverse = inv_s[head, pl.ds(0, 1), :]
            grad = (dot_s[rows, :] * inverse).astype(BF16)
            blank = jnp.zeros_like(grad)
            grad = jnp.concatenate([blank, grad] if odd else [grad, blank], axis=0)
            po, ph = po_s[head], ph_s[head, pl.ds(0, reach), pl.ds(0, reach)]
            own = po.astype(F32) * dot(vo_pair, grad)
            halo = ph.astype(F32) * dot(vh_pair, grad[:, :reach])
            inner = inverse * joined(
                jnp.sum(own, axis=0, keepdims=True),
                jnp.sum(halo, axis=0, keepdims=True),
                reach,
                jnp.add,
            )
            own = (own - po.astype(F32) * inner).astype(BF16)
            halo = (halo - ph.astype(F32) * inner[:, :reach]).astype(BF16)
            dv_own.append(dot(po, grad, NT))
            dv_halo.append(dot(ph, grad[:, :reach], NT))
            dk_own.append(dot(own, q_pair))
            dk_halo.append(dot(halo, q_pair[:reach]))
            dqt = joined(
                dot(kt_s[rows, :], own),
                dot(kht_s[rows, pl.ds(0, reach)], halo),
                reach,
                jnp.add,
            )
            dqt_s[rows, :] = (dqt * (1.0 / math.sqrt(DH))).astype(BF16)
        unscale = 1.0 / LOG2_E
        dv_s[:, lanes] = (dv_own[0] + dv_own[1]).astype(BF16)
        halo_s[pl.ds(tokens, reach), lanes] = (dv_halo[0] + dv_halo[1]).astype(BF16)
        dk_s[:, lanes] = (
            jnp.where(low_half, dk_own[0], dk_own[1]) * unscale
        ).astype(BF16)
        halo_s[pl.ds(0, reach), lanes] = (
            jnp.where(low_half[:reach], dk_halo[0], dk_halo[1]) * unscale
        ).astype(BF16)

    def for_pairs(step):
        @pl.when(jnp.logical_not(wide))
        def _():
            for pair in range(heads // 2):
                step(pair, half)

        @pl.when(wide)
        def _():
            lax.fori_loop(0, heads // 2, lambda pair, none: step(pair, tokens), None)

    for_pairs(attend)

    for copy in get_o:
        copy.wait()
    resid_one = x_ref[...].astype(F32) + dot(ct_s[...], wo[...], TN)
    normal, inverse = normed(resid_one)
    normal_s[...] = normal
    rstd_s[...] = jnp.broadcast_to(inverse, rstd_s.shape)
    gain_one, shift_one = gain_one_s[...].reshape(1, width), shift_one_s[...].reshape(1, width)
    gain_two, shift_two = gain_two_s[...].reshape(1, width), shift_two_s[...].reshape(1, width)
    hidden_one = normal * gain_one + shift_one
    hidden_s[...] = hidden_one.astype(BF16)
    total_s[...] = hidden_one
    for copy in get_u + get_d:
        copy.wait()
    for c in range(chunks):
        part = pl.ds(c * width, width)
        upward = dot(hidden_s[...], wu[:, part])
        value, slope = gelu_and_slope(upward)
        active_s[:, part] = value.astype(BF16)
        slope_s[:, part] = slope.astype(BF16)
        total_s[...] += dot(active_s[:, part], wd[part, :])
    normal_two, inverse_two = normed(total_s[...])
    out_s[...] = (normal_two * gain_two + shift_two).astype(BF16)

    def put(source, target):
        return fetch(source, target)

    puts = [
        put(out_s.at[pl.ds(0, half)], out_hbm.at[0, pl.ds(near, half)]),
        put(out_s.at[pl.ds(half, half)], out_hbm.at[0, pl.ds(far, half)]),
    ]
    for copy in get_cot:
        copy.wait()
    grad_out = cot_s[...].astype(F32)
    grad_gain_two = jnp.sum(grad_out * normal_two, axis=0, keepdims=True)
    grad_shift_two = jnp.sum(grad_out, axis=0, keepdims=True)
    grad_two = norm_back(grad_out * gain_two, normal_two, inverse_two)
    hidden_s[...] = grad_two.astype(BF16)
    total_s[...] = grad_two
    for c in range(chunks):
        part = pl.ds(c * width, width)
        grad_up = slope_s[:, part].astype(F32) * dot(hidden_s[...], wd[part, :], NT)
        active_s[:, part] = grad_up.astype(BF16)
        total_s[...] += dot(active_s[:, part], wu[:, part], NT)
    grad_hidden = total_s[...]
    normal = normal_s[...]
    grad_gain_one = jnp.sum(grad_hidden * normal, axis=0, keepdims=True)
    grad_shift_one = jnp.sum(grad_hidden, axis=0, keepdims=True)
    grad_one = norm_back(grad_hidden * gain_one, normal, rstd_s[:, :1])
    gr_s[...] = grad_one
    dot_s[...] = dot(wo[...], grad_one.astype(BF16), NT)

    @pl.when(jnp.logical_not(wide))
    def _():
        halo_s[pl.ds(half, half)] = jnp.zeros((half, width), BF16)
        halo_s[pl.ds(tokens + half, half)] = jnp.zeros((half, width), BF16)

    for_pairs(attend_back)

    dv_halo = halo_s[pl.ds(tokens, tokens)]
    x_own = x_ref[...]
    grad_qlow_t = (2.0 * dot(bq, dqt_s[...])).astype(BF16)
    grad_vlow_t = (2.0 * dot(bv, dv_s[...], NT)).astype(BF16)
    grad_halo_t = (2.0 * dot(bv, dv_halo, NT)).astype(BF16)
    rows = [
        dot(grad_qlow_t, x_own),
        2.0 * dot(qlow_t, dqt_s[...], NT),
        dot(grad_vlow_t, x_own) + dot(grad_halo_t, x_s[...]),
        2.0 * (dot(vlow_t, dv_s[...]) + dot(halo_low_t, dv_halo)),
        grad_gain_one,
        grad_shift_one,
        grad_gain_two,
        grad_shift_two,
    ]
    spare = packed_ref.shape[0] - 4 * rank - 4
    rows.append(jnp.zeros((spare, width), F32))
    packed_ref[...] = jnp.concatenate(rows, axis=0).astype(BF16)
    for copy in puts:
        copy.wait()


def call_layer(lengths, projected, other, gains, wo, wu, wd, cotangent):
    _, tokens, width = other.shape
    hidden = wu.shape[1]
    heads = width // DH
    rank = projected[-1].shape[0]
    packed_rows = -(-(4 * rank + 4) // 16) * 16
    hbm = pl.BlockSpec(memory_space=pltpu.HBM)
    here = pl.BlockSpec(memory_space=pltpu.VMEM)
    shape = jax.ShapeDtypeStruct
    vmem = pltpu.VMEM
    return pl.pallas_call(
        layer_kernel,
        out_shape=(
            shape((1, tokens, width), BF16),
            shape((tokens, width), F32),
            shape((width, tokens), BF16),
            shape((tokens, width), BF16),
            shape((tokens, width), BF16),
            shape((2 * tokens, width), BF16),
            shape((packed_rows, width), BF16),
        ),
        in_specs=[pl.BlockSpec(memory_space=pltpu.SMEM)] + [here] * 14 + [hbm] * 8,
        out_specs=(hbm,) + (here,) * 6,
        scratch_shapes=[
            vmem((width,), F32),
            vmem((width,), F32),
            vmem((width,), F32),
            vmem((width,), F32),
            vmem((tokens, width), BF16),
            vmem(wo.shape, BF16),
            vmem(wu.shape, BF16),
            vmem(wd.shape, BF16),
            vmem((tokens, width), BF16),
            vmem((tokens, width), BF16),
            vmem((tokens, width), BF16),
            vmem((width, tokens), BF16),
            vmem((width, tokens), BF16),
            vmem((heads, tokens, tokens), BF16),
            vmem((heads, tokens, tokens), BF16),
            vmem((heads, 8, tokens), F32),
            vmem((width, tokens), BF16),
            vmem((tokens, width), F32),
            vmem((tokens, LANES), F32),
            vmem((tokens, width), BF16),
            vmem((tokens, hidden), BF16),
            vmem((tokens, hidden), BF16),
            vmem((tokens, width), F32),
            vmem((tokens, width), BF16),
            vmem((width, tokens), F32),
            pltpu.SemaphoreType.DMA((32,)),
        ],
        compiler_params=pltpu.CompilerParams(vmem_limit_bytes=44 * 2**20),
        cost_estimate=pl.CostEstimate(flops=9 * 10**9, bytes_accessed=15 * 10**6, transcendentals=0),
    )(lengths, *projected, other, *in_hbm(*gains, wo, wu, wd, cotangent))


def inputs_kernel(
    halo_ref,
    gr,
    dqt,
    dk,
    dv,
    wq_hbm,
    wk_hbm,
    wv_hbm,
    aqt_hbm,
    bq_hbm,
    avt_hbm,
    bv_hbm,
    out_hbm,
    wq,
    wk,
    wv,
    aqt,
    bq,
    avt,
    bv,
    out_s,
    sems,
):
    tokens, width = gr.shape
    half = tokens // 2
    near, far = own_rows(lax.axis_index("seq"), half)
    pairs = (
        (wq_hbm, wq),
        (wk_hbm, wk),
        (wv_hbm, wv),
        (bq_hbm, bq),
        (aqt_hbm, aqt),
        (bv_hbm, bv),
        (avt_hbm, avt),
    )
    copies = [pltpu.make_async_copy(a, b, sems.at[i]) for i, (a, b) in enumerate(pairs)]
    for copy in copies:
        copy.start()
    for copy in copies:
        copy.wait()
    grad_k = (dk[...].astype(F32) + halo_ref[pl.ds(0, tokens)].astype(F32)).astype(BF16)
    grad_v = (dv[...].astype(F32) + halo_ref[pl.ds(tokens, tokens)].astype(F32)).astype(BF16)
    grad_qlow_t = (2.0 * dot(bq[...], dqt[...])).astype(BF16)
    grad_vlow_t = (2.0 * dot(bv[...], grad_v, NT)).astype(BF16)
    out_s[...] = (
        gr[...]
        + dot(dqt[...], wq[...], TT)
        + dot(grad_k, wk[...], NT)
        + dot(grad_v, wv[...], NT)
        + dot(grad_qlow_t, aqt[...], TN)
        + dot(grad_vlow_t, avt[...], TN)
    )
    puts = [
        pltpu.make_async_copy(
            out_s.at[pl.ds(0, half)], out_hbm.at[0, pl.ds(near, half)], sems.at[11]
        ),
        pltpu.make_async_copy(
            out_s.at[pl.ds(half, half)], out_hbm.at[0, pl.ds(far, half)], sems.at[12]
        ),
    ]
    for copy in puts:
        copy.start()
    for copy in puts:
        copy.wait()


def call_inputs(halo, gr, dqt, dk, dv, wq, wk, wv, lows):
    tokens, width = gr.shape
    weights = (wq, wk, wv, *lows)
    return pl.pallas_call(
        inputs_kernel,
        out_shape=jax.ShapeDtypeStruct((1, tokens, width), F32),
        in_specs=[pl.BlockSpec(memory_space=pltpu.VMEM)] * 5
        + [pl.BlockSpec(memory_space=pltpu.HBM)] * len(weights),
        out_specs=pl.BlockSpec(memory_space=pltpu.HBM),
        scratch_shapes=[pltpu.VMEM(a.shape, a.dtype) for a in weights]
        + [pltpu.VMEM((tokens, width), F32), pltpu.SemaphoreType.DMA((13,))],
        compiler_params=pltpu.CompilerParams(vmem_limit_bytes=10 * 2**20),
        cost_estimate=pl.CostEstimate(flops=2 * 10**9, bytes_accessed=6 * 10**6, transcendentals=0),
    )(halo, gr, dqt, dk, dv, *in_hbm(*weights))


def finish_kernel(rank, count, *refs):
    ins, outs = refs[:count], refs[count : count + 8]
    scratch, singles, sems = refs[-6], refs[-5:-1], refs[-1]
    total = ins[0][...].astype(F32)
    for one in ins[1:]:
        total = total + one[...].astype(F32)
    scratch[...] = total
    copies = []
    for i, out in enumerate(outs):
        if i < 4:
            source = scratch.at[pl.ds(i * rank, rank)]
        else:
            source = singles[i - 4]
            source[...] = total[4 * rank + i - 4]
        copies.append(pltpu.make_async_copy(source, out, sems.at[i]))
    for copy in copies:
        copy.start()
    for copy in copies:
        copy.wait()


def call_finish(rank, parts):
    rows, width = parts[0].shape
    shape = jax.ShapeDtypeStruct
    return pl.pallas_call(
        functools.partial(finish_kernel, rank, len(parts)),
        out_shape=(shape((rank, width), F32),) * 4 + (shape((width,), F32),) * 4,
        in_specs=[pl.BlockSpec(memory_space=pltpu.VMEM)] * len(parts),
        out_specs=(pl.BlockSpec(memory_space=pltpu.HBM),) * 8,
        scratch_shapes=[pltpu.VMEM((rows, width), F32)]
        + [pltpu.VMEM((width,), F32)] * 4
        + [pltpu.SemaphoreType.DMA((8,))],
        compiler_params=pltpu.CompilerParams(vmem_limit_bytes=4 * 2**20),
    )(*parts)


def swapped(values, axis, partners):
    size = lax.axis_size(axis)
    return [values] + [
        lax.ppermute(values, axis, [(i, i ^ p) for i in range(size)]) for p in partners
    ]


def added(parts):
    total = parts[0].astype(F32)
    for one in parts[1:]:
        total = total + one.astype(F32)
    return total.astype(BF16)


def parts_of_sum(values, beside):
    parts = swapped(values, "seq", (1,))
    stride, size = 1, lax.axis_size("dp")
    while stride < size:
        radix = min(4, size // stride)
        parts = swapped(added(parts), "dp", [stride * k for k in range(1, radix)])
        if stride == 1:
            *parts, beside = lax.optimization_barrier((*parts, beside))
        stride *= radix
    return parts, beside


def body(
    inputs,
    pair_lengths,
    w_query,
    w_key,
    w_value,
    w_out,
    w_up,
    w_down,
    a_query,
    b_query,
    a_value,
    b_value,
    gain_one,
    shift_one,
    gain_two,
    shift_two,
    cotangent,
):
    rank = a_query.shape[1]
    swap = [(0, 1), (1, 0)]
    other = lax.ppermute(inputs, "seq", swap)
    lows = (a_query.T, b_query, a_value.T, b_value)
    gains = (gain_one, shift_one, gain_two, shift_two)
    projected = call_project(inputs, w_query, w_key, w_value, lows)
    output, gr, dqt, dk, dv, halo, packed = call_layer(
        pair_lengths, projected, other, gains, w_out, w_up, w_down, cotangent
    )
    halo = lax.ppermute(halo, "seq", swap)
    grad_inputs = call_inputs(halo, gr, dqt, dk, dv, w_query, w_key, w_value, lows)
    parts, grad_inputs = parts_of_sum(packed, grad_inputs)
    gaq, gbq, gav, gbv, *norms = call_finish(rank, parts)
    return (output, grad_inputs, gaq.T, gbq, gav.T, gbv, *norms)


def solution(mesh):
    tokens = P("dp", "seq", None)
    in_specs = (tokens, P("dp", None)) + (P(),) * 14 + (tokens,)
    out_specs = (tokens, tokens) + (P(),) * 8
    return jax.shard_map(body, mesh=mesh, in_specs=in_specs, out_specs=out_specs, check_vma=False)
```

```python
import functools
import math

import jax
import jax.numpy as jnp
from jax import lax
from jax.experimental import pallas as pl
from jax.experimental.pallas import tpu as pltpu
from jax.sharding import PartitionSpec as P

DH = 64
LANES = 128
EARLY = 3
EPSILON = 1e-05
LOG2_E = math.log2(math.e)
FAR_AWAY = -1e30
BF16 = jnp.bfloat16
F32 = jnp.float32
NN = ((1,), (0,))
NT = ((1,), (1,))
TN = ((0,), (0,))
TT = ((0,), (1,))


def dot(former, latter, dims=NN):
    return lax.dot_general(former, latter, (dims, ((), ())), preferred_element_type=F32)


def normed(values):
    centred = values - jnp.mean(values, axis=-1, keepdims=True)
    variance = jnp.mean(centred * centred, axis=-1, keepdims=True)
    inverse = lax.rsqrt(variance + EPSILON)
    return centred * inverse, inverse


def norm_back(grad, normal, inverse):
    return inverse * (
        grad
        - jnp.mean(grad, axis=-1, keepdims=True)
        - normal * jnp.mean(grad * normal, axis=-1, keepdims=True)
    )


def gelu_and_slope(values):
    below = 0.5 + 0.5 * lax.erf(values * (1.0 / math.sqrt(2.0)))
    bell = jnp.exp2(values * values * (-0.5 * LOG2_E))
    return values * below, below + values * bell * (1.0 / math.sqrt(2.0 * math.pi))


def segment_codes(lengths_ref, start_near, start_far, rows):
    row = lax.broadcasted_iota(jnp.int32, (rows, LANES), 0)
    half = rows // 2
    place = jnp.where(row < half, start_near + row, start_far + row - half)
    segment = jnp.zeros_like(place)
    end = jnp.int32(0)
    for pair in range(lengths_ref.shape[1]):
        end = end + lengths_ref[0, pair]
        segment = segment + (place >= end).astype(jnp.int32)
    return segment


def crosses_widely(lengths_ref, middle, half):
    end = jnp.int32(0)
    left = jnp.int32(middle)
    right = jnp.int32(middle)
    for pair in range(lengths_ref.shape[1]):
        end = end + lengths_ref[0, pair]
        left = jnp.where(end < middle, middle - end, left)
        right = jnp.where(end >= middle, jnp.minimum(right, end - middle), right)
    return (right > 0) & ((left > half) | (right > half))


def in_hbm(*arrays):
    return [pltpu.with_memory_space_constraint(a, pltpu.HBM) for a in arrays]


def own_rows(side, half):
    return pl.multiple_of((1 - side) * half, half), pl.multiple_of(side * half, half)


def project_kernel(
    x_hbm,
    wq_hbm,
    wk_hbm,
    wv_hbm,
    aqt_hbm,
    bq_hbm,
    avt_hbm,
    bv_hbm,
    wo_hbm,
    wu_hbm,
    x_ref,
    q_ref,
    k_ref,
    v_ref,
    kt_ref,
    vt_ref,
    qlow_ref,
    vlow_ref,
    wk,
    wv,
    bq,
    avt,
    bv,
    wo,
    wu,
    wq,
    aqt,
    sems,
):
    tokens = x_hbm.shape[1]
    half = tokens // 2
    near, far = own_rows(lax.axis_index("seq"), half)
    pairs = (
        (x_hbm.at[0, pl.ds(near, half)], x_ref.at[pl.ds(0, half)]),
        (x_hbm.at[0, pl.ds(far, half)], x_ref.at[pl.ds(half, half)]),
        (wk_hbm, wk),
        (aqt_hbm, aqt),
        (bq_hbm, bq),
        (avt_hbm, avt),
        (bv_hbm, bv),
        (wq_hbm, wq),
        (wv_hbm, wv),
        (wo_hbm, wo),
        (wu_hbm.at[:, pl.ds(0, wu.shape[1])], wu),
    )
    copies = [pltpu.make_async_copy(a, b, sems.at[i]) for i, (a, b) in enumerate(pairs)]
    for copy in copies:
        copy.start()
    for copy in copies[:3]:
        copy.wait()
    x = x_ref[...]
    keys = dot(x, wk[...]).astype(BF16)
    k_ref[...] = keys
    kt_ref[...] = keys.T
    for copy in copies[3:9]:
        copy.wait()
    qlow_t = dot(aqt[...], x, NT).astype(BF16)
    vlow_t = dot(avt[...], x, NT).astype(BF16)
    qlow_ref[...] = qlow_t
    vlow_ref[...] = vlow_t
    q_ref[...] = (
        (dot(x, wq[...]) + 2.0 * dot(qlow_t, bq[...], TN)) * (LOG2_E / math.sqrt(DH))
    ).astype(BF16)
    vals = (dot(x, wv[...]) + 2.0 * dot(vlow_t, bv[...], TN)).astype(BF16)
    v_ref[...] = vals
    vt_ref[...] = vals.T
    for copy in copies[9:]:
        copy.wait()


def call_project(x, wq, wk, wv, lows, wo, wu):
    _, tokens, width = x.shape
    rank = lows[1].shape[0]
    shape = jax.ShapeDtypeStruct
    rows, columns = shape((tokens, width), BF16), shape((width, tokens), BF16)
    low = shape((rank, tokens), BF16)
    square, flat = shape((width, width), BF16), shape((rank, width), BF16)
    return pl.pallas_call(
        project_kernel,
        out_shape=(rows,) * 4
        + (columns,) * 2
        + (low,) * 2
        + (square,) * 2
        + (flat,) * 3
        + (square, shape((width, EARLY * width), BF16)),
        in_specs=[pl.BlockSpec(memory_space=pltpu.HBM)] * 10,
        out_specs=(pl.BlockSpec(memory_space=pltpu.VMEM),) * 15,
        scratch_shapes=[
            pltpu.VMEM((width, width), BF16),
            pltpu.VMEM((rank, width), BF16),
            pltpu.SemaphoreType.DMA((11,)),
        ],
        compiler_params=pltpu.CompilerParams(vmem_limit_bytes=20 * 2**20),
        cost_estimate=pl.CostEstimate(flops=10**9, bytes_accessed=8 * 10**6, transcendentals=0),
    )(*in_hbm(x, wq, wk, wv, *lows, wo, wu))


def layer_kernel(
    lengths_ref,
    x_ref,
    q_s,
    k_s,
    v_s,
    kt_s,
    vt_s,
    qlow_ref,
    vlow_ref,
    wk,
    wv,
    bq_ref,
    avt_ref,
    bv_ref,
    wo,
    wu_early,
    other_ref,
    gain_one_hbm,
    shift_one_hbm,
    gain_two_hbm,
    shift_two_hbm,
    wu_hbm,
    wd_hbm,
    cot_hbm,
    out_hbm,
    gr_s,
    dqt_s,
    dk_s,
    dv_s,
    halo_s,
    packed_ref,
    gain_one_s,
    shift_one_s,
    gain_two_s,
    shift_two_s,
    x_s,
    wu_late,
    wd,
    cot_s,
    kh_s,
    vh_s,
    kht_s,
    vht_s,
    p_s,
    inv_s,
    ct_s,
    normal_s,
    rstd_s,
    hidden_s,
    active_s,
    slope_s,
    total_s,
    out_s,
    dot_s,
    sems,
):
    tokens, width = x_ref.shape
    half = tokens // 2
    hidden = wu_hbm.shape[1]
    rank = bq_ref.shape[0]
    heads = width // DH
    side = lax.axis_index("seq")
    near, far = own_rows(side, half)

    copies = []

    def fetch(source, target):
        copy = pltpu.make_async_copy(source, target, sems.at[len(copies)])
        copies.append(copy)
        copy.start()
        return copy

    get_gains = [
        fetch(gain_one_hbm, gain_one_s),
        fetch(shift_one_hbm, shift_one_s),
        fetch(gain_two_hbm, gain_two_s),
        fetch(shift_two_hbm, shift_two_s),
    ]
    chunks = hidden // width
    early = wu_early.shape[1]
    get_ffn = [fetch(wu_hbm.at[:, pl.ds(early, hidden - early)], wu_late)]
    for c in range(chunks):
        part = pl.ds(c * width, width)
        get_ffn.append(fetch(wd_hbm.at[part], wd.at[part]))

    def wu_part(c):
        start = c * width
        if start < early:
            return wu_early[:, pl.ds(start, width)]
        return wu_late[:, pl.ds(start - early, width)]

    get_cot = [
        fetch(cot_hbm.at[0, pl.ds(near, half)], cot_s.at[pl.ds(0, half)]),
        fetch(cot_hbm.at[0, pl.ds(far, half)], cot_s.at[pl.ds(half, half)]),
    ]

    wide = crosses_widely(lengths_ref, tokens, half)
    own_segment = segment_codes(lengths_ref, side * tokens + near, side * tokens + far, tokens)
    halo_base = (1 - side) * tokens
    halo_segment = segment_codes(lengths_ref, halo_base + far, halo_base + near, tokens)
    lane = lax.broadcasted_iota(jnp.int32, (tokens, LANES), 1)
    code = lane & (DH - 1)
    low_lanes = lax.broadcasted_iota(jnp.int32, (2 * tokens, LANES), 1) < DH
    marks = lengths_ref.shape[1] + 1
    q_code = jnp.where(code == own_segment, 1.0, 0.0).astype(BF16)

    def key_code(segment):
        return jnp.where((code < marks) & (code != segment), FAR_AWAY, 0.0).astype(BF16)

    ko_code = key_code(own_segment)
    kh_code = key_code(halo_segment)

    bq, avt, bv = bq_ref[...], avt_ref[...], bv_ref[...]
    qlow_t, vlow_t = qlow_ref[...], vlow_ref[...]
    x_s[pl.ds(0, half)] = other_ref[0, pl.ds(far, half)]
    x_s[pl.ds(half, half)] = other_ref[0, pl.ds(near, half)]
    halo_low_t = dot(avt, x_s[...], NT).astype(BF16)

    def project_halo(start):
        rows = pl.ds(start, half)
        x_halo = x_s[rows]
        keys = dot(x_halo, wk[...]).astype(BF16)
        kh_s[rows] = keys
        kht_s[:, rows] = keys.T
        low_t = halo_low_t[:, start : start + half]
        vals = (dot(x_halo, wv[...]) + 2.0 * dot(low_t, bv, TN)).astype(BF16)
        vh_s[rows] = vals
        vht_s[:, rows] = vals.T

    project_halo(0)

    @pl.when(wide)
    def _():
        project_halo(half)

    def joined(own, halo, reach, join):
        if reach == tokens:
            return join(own, halo)
        return jnp.concatenate([join(own[:, :reach], halo), own[:, reach:]], axis=1)

    def padded(halo, reach):
        if reach == tokens:
            return halo
        return jnp.concatenate([halo, jnp.zeros((reach, tokens - reach), halo.dtype)], axis=1)

    def lanes_of(pair):
        return pl.ds(pl.multiple_of(pair * LANES, LANES), LANES)

    def rows_of(pair, odd):
        return pl.ds(pl.multiple_of(pair * LANES + odd * DH, DH), DH)

    def score(pair, odd, reach):
        lanes = lanes_of(pair)

        def mixed(values, codes):
            mask = low_lanes[: values.shape[0]]
            if odd:
                return jnp.where(mask, codes, values)
            return jnp.where(mask, values, codes)

        k_pair = jnp.concatenate([k_s[:, lanes], kh_s[pl.ds(0, reach), lanes]], axis=0)
        k_code = jnp.concatenate([ko_code, kh_code[:reach]], axis=0)
        return dot(mixed(k_pair, k_code), mixed(q_s[:, lanes], q_code), NT)

    def soften(pair, odd, reach, scores):
        head = 2 * pair + odd
        own, halo = scores[:tokens], scores[tokens:, :reach]
        peak = joined(
            jnp.max(own, axis=0, keepdims=True),
            jnp.max(halo, axis=0, keepdims=True),
            reach,
            jnp.maximum,
        )
        own = jnp.exp2(own - peak)
        halo = jnp.exp2(halo - peak[:, :reach])
        inverse = 1.0 / joined(
            jnp.sum(own, axis=0, keepdims=True),
            jnp.sum(halo, axis=0, keepdims=True),
            reach,
            jnp.add,
        )
        own, halo = own.astype(BF16), padded(halo.astype(BF16), reach)
        p_s[head, pl.ds(0, tokens)] = own
        p_s[head, pl.ds(tokens, reach)] = halo
        inv_s[head] = jnp.broadcast_to(inverse, inv_s.shape[1:])
        return own, halo, inverse

    def attend(pair, odd, reach, soft):
        own, halo, inverse = soft
        rows = rows_of(pair, odd)
        context = dot(vt_s[rows, :], own) + dot(vht_s[rows, pl.ds(0, reach)], halo)
        ct_s[rows, :] = (context * inverse).astype(BF16)

    def back_score(pair, odd, reach):
        lanes = lanes_of(pair)
        inverse = inv_s[2 * pair + odd, pl.ds(0, 1), :]
        grad = (dot_s[rows_of(pair, odd), :] * inverse).astype(BF16)
        blank = jnp.zeros_like(grad)
        grad = jnp.concatenate([blank, grad] if odd else [grad, blank], axis=0)
        own = dot(v_s[:, lanes], grad)
        halo = dot(vh_s[pl.ds(0, reach), lanes], grad[:, :reach])
        return inverse, grad, own, halo

    evens = {}

    def back_soften(pair, odd, reach, slopes):
        head = 2 * pair + odd
        inverse, grad, own, halo = slopes
        p_own, p_halo = p_s[head, pl.ds(0, tokens)], p_s[head, pl.ds(tokens, reach), pl.ds(0, reach)]
        po, ph = p_own.astype(F32), p_halo.astype(F32)
        own, halo = po * own, ph * halo
        inner = inverse * joined(
            jnp.sum(own, axis=0, keepdims=True),
            jnp.sum(halo, axis=0, keepdims=True),
            reach,
            jnp.add,
        )
        own = (own - po * inner).astype(BF16)
        halo = (halo - ph * inner[:, :reach]).astype(BF16)
        return grad, p_own, p_halo, own, halo

    def attend_back(pair, odd, reach, soft):
        lanes, rows = lanes_of(pair), rows_of(pair, odd)
        grad, p_own, p_halo, own, halo = soft
        q_pair = q_s[:, lanes]
        parts = (
            dot(p_own, grad, NT),
            dot(p_halo, grad[:, :reach], NT),
            dot(own, q_pair),
            dot(halo, q_pair[:reach]),
        )
        dq = joined(
            dot(kt_s[rows, :], own),
            dot(kht_s[rows, pl.ds(0, reach)], halo),
            reach,
            jnp.add,
        )
        dqt_s[rows, :] = (dq * (1.0 / math.sqrt(DH))).astype(BF16)
        if not odd:
            evens[0] = parts
            return
        even = evens.pop(0)
        unscale = 1.0 / LOG2_E
        dv_s[:, lanes] = (even[0] + parts[0]).astype(BF16)
        halo_s[pl.ds(tokens, reach), lanes] = (even[1] + parts[1]).astype(BF16)
        dk_s[:, lanes] = (
            jnp.where(low_lanes[:tokens], even[2], parts[2]) * unscale
        ).astype(BF16)
        halo_s[pl.ds(0, reach), lanes] = (
            jnp.where(low_lanes[:reach], even[3], parts[3]) * unscale
        ).astype(BF16)

    def for_heads(first, second, third, lags):
        @pl.when(jnp.logical_not(wide))
        def _():
            todo = [(pair, odd) for pair in range(heads // 2) for odd in range(2)]
            one, two = {}, {}
            for at in range(len(todo) + lags[1]):
                if at < len(todo):
                    one[at] = first(*todo[at], half)
                back = at - lags[0]
                if 0 <= back < len(todo):
                    two[back] = second(*todo[back], half, one.pop(back))
                back = at - lags[1]
                if 0 <= back:
                    third(*todo[back], half, two.pop(back))

        @pl.when(wide)
        def _():
            def step(pair, none):
                for odd in range(2):
                    third(
                        pair,
                        odd,
                        tokens,
                        second(pair, odd, tokens, first(pair, odd, tokens)),
                    )

            lax.fori_loop(0, heads // 2, step, None)

    for_heads(score, soften, attend, (2, 4))

    for copy in get_gains:
        copy.wait()
    resid_one = x_ref[...].astype(F32) + dot(ct_s[...], wo[...], TN)
    normal, inverse = normed(resid_one)
    normal_s[...] = normal
    rstd_s[...] = jnp.broadcast_to(inverse, rstd_s.shape)
    gain_one, shift_one = gain_one_s[...].reshape(1, width), shift_one_s[...].reshape(1, width)
    gain_two, shift_two = gain_two_s[...].reshape(1, width), shift_two_s[...].reshape(1, width)
    hidden_one = normal * gain_one + shift_one
    hidden_s[...] = hidden_one.astype(BF16)
    total_s[...] = hidden_one
    for copy in get_ffn:
        copy.wait()
    for c in range(chunks):
        part = pl.ds(c * width, width)
        upward = dot(hidden_s[...], wu_part(c))
        value, slope = gelu_and_slope(upward)
        active_s[:, part] = value.astype(BF16)
        slope_s[:, part] = slope.astype(BF16)
        total_s[...] += dot(active_s[:, part], wd[part, :])
    normal_two, inverse_two = normed(total_s[...])
    out_s[...] = (normal_two * gain_two + shift_two).astype(BF16)

    def put(source, target):
        return fetch(source, target)

    puts = [
        put(out_s.at[pl.ds(0, half)], out_hbm.at[0, pl.ds(near, half)]),
        put(out_s.at[pl.ds(half, half)], out_hbm.at[0, pl.ds(far, half)]),
    ]
    for copy in get_cot:
        copy.wait()
    grad_out = cot_s[...].astype(F32)
    grad_gain_two = jnp.sum(grad_out * normal_two, axis=0, keepdims=True)
    grad_shift_two = jnp.sum(grad_out, axis=0, keepdims=True)
    grad_two = norm_back(grad_out * gain_two, normal_two, inverse_two)
    hidden_s[...] = grad_two.astype(BF16)
    total_s[...] = grad_two
    for c in range(chunks):
        part = pl.ds(c * width, width)
        grad_up = slope_s[:, part].astype(F32) * dot(hidden_s[...], wd[part, :], NT)
        active_s[:, part] = grad_up.astype(BF16)
        total_s[...] += dot(active_s[:, part], wu_part(c), NT)
    grad_hidden = total_s[...]
    normal = normal_s[...]
    grad_gain_one = jnp.sum(grad_hidden * normal, axis=0, keepdims=True)
    grad_shift_one = jnp.sum(grad_hidden, axis=0, keepdims=True)
    grad_one = norm_back(grad_hidden * gain_one, normal, rstd_s[:, :1])
    gr_s[...] = grad_one
    dot_s[...] = dot(wo[...], grad_one.astype(BF16), NT)

    @pl.when(jnp.logical_not(wide))
    def _():
        halo_s[pl.ds(half, half)] = jnp.zeros((half, width), BF16)
        halo_s[pl.ds(tokens + half, half)] = jnp.zeros((half, width), BF16)

    for_heads(back_score, back_soften, attend_back, (2, 4))

    dv_halo = halo_s[pl.ds(tokens, tokens)]
    x_own = x_ref[...]
    grad_qlow_t = (2.0 * dot(bq, dqt_s[...])).astype(BF16)
    grad_vlow_t = (2.0 * dot(bv, dv_s[...], NT)).astype(BF16)
    grad_halo_t = (2.0 * dot(bv, dv_halo, NT)).astype(BF16)
    rows = [
        dot(grad_qlow_t, x_own),
        2.0 * dot(qlow_t, dqt_s[...], NT),
        dot(grad_vlow_t, x_own) + dot(grad_halo_t, x_s[...]),
        2.0 * (dot(vlow_t, dv_s[...]) + dot(halo_low_t, dv_halo)),
        grad_gain_one,
        grad_shift_one,
        grad_gain_two,
        grad_shift_two,
    ]
    spare = packed_ref.shape[0] - 4 * rank - 4
    rows.append(jnp.zeros((spare, width), F32))
    packed_ref[...] = jnp.concatenate(rows, axis=0).astype(BF16)
    for copy in puts:
        copy.wait()


def call_layer(lengths, projected, other, gains, wu, wd, cotangent):
    _, tokens, width = other.shape
    hidden = wu.shape[1]
    heads = width // DH
    rank = projected[6].shape[0]
    packed_rows = -(-(4 * rank + 4) // 8) * 8
    hbm = pl.BlockSpec(memory_space=pltpu.HBM)
    here = pl.BlockSpec(memory_space=pltpu.VMEM)
    shape = jax.ShapeDtypeStruct
    vmem = pltpu.VMEM
    return pl.pallas_call(
        layer_kernel,
        out_shape=(
            shape((1, tokens, width), BF16),
            shape((tokens, width), F32),
            shape((width, tokens), BF16),
            shape((tokens, width), BF16),
            shape((tokens, width), BF16),
            shape((2 * tokens, width), BF16),
            shape((packed_rows, width), BF16),
        ),
        in_specs=[pl.BlockSpec(memory_space=pltpu.SMEM)] + [here] * 16 + [hbm] * 7,
        out_specs=(hbm,) + (here,) * 6,
        scratch_shapes=[
            vmem((width,), F32),
            vmem((width,), F32),
            vmem((width,), F32),
            vmem((width,), F32),
            vmem((tokens, width), BF16),
            vmem((width, hidden - EARLY * width), BF16),
            vmem(wd.shape, BF16),
            vmem((tokens, width), BF16),
            vmem((tokens, width), BF16),
            vmem((tokens, width), BF16),
            vmem((width, tokens), BF16),
            vmem((width, tokens), BF16),
            vmem((heads, 2 * tokens, tokens), BF16),
            vmem((heads, 8, tokens), F32),
            vmem((width, tokens), BF16),
            vmem((tokens, width), F32),
            vmem((tokens, LANES), F32),
            vmem((tokens, width), BF16),
            vmem((tokens, hidden), BF16),
            vmem((tokens, hidden), BF16),
            vmem((tokens, width), F32),
            vmem((tokens, width), BF16),
            vmem((width, tokens), F32),
            pltpu.SemaphoreType.DMA((32,)),
        ],
        compiler_params=pltpu.CompilerParams(vmem_limit_bytes=36 * 2**20),
        cost_estimate=pl.CostEstimate(flops=9 * 10**9, bytes_accessed=15 * 10**6, transcendentals=0),
    )(lengths, *projected, other, *in_hbm(*gains, wu, wd, cotangent))


def inputs_kernel(
    halo_ref,
    gr,
    dqt,
    dk,
    dv,
    wq_hbm,
    wk_hbm,
    wv_hbm,
    aqt_hbm,
    bq_hbm,
    avt_hbm,
    bv_hbm,
    out_hbm,
    wq,
    wk,
    wv,
    aqt,
    bq,
    avt,
    bv,
    out_s,
    sems,
):
    tokens, width = gr.shape
    half = tokens // 2
    near, far = own_rows(lax.axis_index("seq"), half)
    pairs = (
        (wq_hbm, wq),
        (wk_hbm, wk),
        (wv_hbm, wv),
        (bq_hbm, bq),
        (aqt_hbm, aqt),
        (bv_hbm, bv),
        (avt_hbm, avt),
    )
    copies = [pltpu.make_async_copy(a, b, sems.at[i]) for i, (a, b) in enumerate(pairs)]
    for copy in copies:
        copy.start()
    for copy in copies:
        copy.wait()
    grad_k = (dk[...].astype(F32) + halo_ref[pl.ds(0, tokens)].astype(F32)).astype(BF16)
    grad_v = (dv[...].astype(F32) + halo_ref[pl.ds(tokens, tokens)].astype(F32)).astype(BF16)
    grad_qlow_t = (2.0 * dot(bq[...], dqt[...])).astype(BF16)
    grad_vlow_t = (2.0 * dot(bv[...], grad_v, NT)).astype(BF16)
    out_s[...] = (
        gr[...]
        + dot(dqt[...], wq[...], TT)
        + dot(grad_k, wk[...], NT)
        + dot(grad_v, wv[...], NT)
        + dot(grad_qlow_t, aqt[...], TN)
        + dot(grad_vlow_t, avt[...], TN)
    )
    puts = [
        pltpu.make_async_copy(
            out_s.at[pl.ds(0, half)], out_hbm.at[0, pl.ds(near, half)], sems.at[11]
        ),
        pltpu.make_async_copy(
            out_s.at[pl.ds(half, half)], out_hbm.at[0, pl.ds(far, half)], sems.at[12]
        ),
    ]
    for copy in puts:
        copy.start()
    for copy in puts:
        copy.wait()


def call_inputs(halo, gr, dqt, dk, dv, wq, wk, wv, lows):
    tokens, width = gr.shape
    weights = (wq, wk, wv, *lows)
    return pl.pallas_call(
        inputs_kernel,
        out_shape=jax.ShapeDtypeStruct((1, tokens, width), F32),
        in_specs=[pl.BlockSpec(memory_space=pltpu.VMEM)] * 5
        + [pl.BlockSpec(memory_space=pltpu.HBM)] * len(weights),
        out_specs=pl.BlockSpec(memory_space=pltpu.HBM),
        scratch_shapes=[pltpu.VMEM(a.shape, a.dtype) for a in weights]
        + [pltpu.VMEM((tokens, width), F32), pltpu.SemaphoreType.DMA((13,))],
        compiler_params=pltpu.CompilerParams(vmem_limit_bytes=10 * 2**20),
        cost_estimate=pl.CostEstimate(flops=2 * 10**9, bytes_accessed=6 * 10**6, transcendentals=0),
    )(halo, gr, dqt, dk, dv, *in_hbm(*weights))


def finish_kernel(rank, count, *refs):
    ins, outs = refs[:count], refs[count : count + 8]
    scratch, singles, sems = refs[-6], refs[-5:-1], refs[-1]
    total = ins[0][...].astype(F32)
    for one in ins[1:]:
        total = total + one[...].astype(F32)
    scratch[...] = total
    copies = []
    for i, out in enumerate(outs):
        if i < 4:
            source = scratch.at[pl.ds(i * rank, rank)]
        else:
            source = singles[i - 4]
            source[...] = total[4 * rank + i - 4]
        copies.append(pltpu.make_async_copy(source, out, sems.at[i]))
    for copy in copies:
        copy.start()
    for copy in copies:
        copy.wait()


def call_finish(rank, parts):
    rows, width = parts[0].shape
    shape = jax.ShapeDtypeStruct
    return pl.pallas_call(
        functools.partial(finish_kernel, rank, len(parts)),
        out_shape=(shape((rank, width), F32),) * 4 + (shape((width,), F32),) * 4,
        in_specs=[pl.BlockSpec(memory_space=pltpu.VMEM)] * len(parts),
        out_specs=(pl.BlockSpec(memory_space=pltpu.HBM),) * 8,
        scratch_shapes=[pltpu.VMEM((rows, width), F32)]
        + [pltpu.VMEM((width,), F32)] * 4
        + [pltpu.SemaphoreType.DMA((8,))],
        compiler_params=pltpu.CompilerParams(vmem_limit_bytes=4 * 2**20),
    )(*parts)


def swapped(values, axis, partners):
    size = lax.axis_size(axis)
    return [values] + [
        lax.ppermute(values, axis, [(i, i ^ p) for i in range(size)]) for p in partners
    ]


def added(parts):
    total = parts[0].astype(F32)
    for one in parts[1:]:
        total = total + one.astype(F32)
    return total.astype(BF16)


def parts_of_sum(values, beside):
    parts = swapped(values, "seq", (1,))
    stride, size = 1, lax.axis_size("dp")
    while stride < size:
        values = added(parts)
        if stride == 1:
            beside, values = lax.optimization_barrier((beside, values))
        radix = min(4, size // stride)
        parts = swapped(values, "dp", [stride * k for k in range(1, radix)])
        stride *= radix
    return parts, beside


def body(
    inputs,
    pair_lengths,
    w_query,
    w_key,
    w_value,
    w_out,
    w_up,
    w_down,
    a_query,
    b_query,
    a_value,
    b_value,
    gain_one,
    shift_one,
    gain_two,
    shift_two,
    cotangent,
):
    rank = a_query.shape[1]
    swap = [(0, 1), (1, 0)]
    other = lax.ppermute(inputs, "seq", swap)
    lows = (a_query.T, b_query, a_value.T, b_value)
    gains = (gain_one, shift_one, gain_two, shift_two)
    projected = call_project(inputs, w_query, w_key, w_value, lows, w_out, w_up)
    output, gr, dqt, dk, dv, halo, packed = call_layer(
        pair_lengths, projected, other, gains, w_up, w_down, cotangent
    )
    parts, halo = parts_of_sum(packed, halo)
    halo = lax.ppermute(halo, "seq", swap)
    grad_inputs = call_inputs(halo, gr, dqt, dk, dv, w_query, w_key, w_value, lows)
    *parts, grad_inputs = lax.optimization_barrier((*parts, grad_inputs))
    gaq, gbq, gav, gbv, *norms = call_finish(rank, parts)
    return (output, grad_inputs, gaq.T, gbq, gav.T, gbv, *norms)


def solution(mesh):
    tokens = P("dp", "seq", None)
    in_specs = (tokens, P("dp", None)) + (P(),) * 14 + (tokens,)
    out_specs = (tokens, tokens) + (P(),) * 8
    return jax.shard_map(body, mesh=mesh, in_specs=in_specs, out_specs=out_specs, check_vma=False)
```

```python
import functools
import math

import jax
import jax.numpy as jnp
from jax import lax
from jax.experimental import pallas as pl
from jax.experimental.pallas import tpu as pltpu
from jax.sharding import PartitionSpec as P

DH = 64
LANES = 128
EARLY = 3
EPSILON = 1e-05
LOG2_E = math.log2(math.e)
FAR_AWAY = -1e30
BF16 = jnp.bfloat16
F32 = jnp.float32
NN = ((1,), (0,))
NT = ((1,), (1,))
TN = ((0,), (0,))
TT = ((0,), (1,))


def dot(former, latter, dims=NN):
    return lax.dot_general(former, latter, (dims, ((), ())), preferred_element_type=F32)


def normed(values):
    centred = values - jnp.mean(values, axis=-1, keepdims=True)
    variance = jnp.mean(centred * centred, axis=-1, keepdims=True)
    inverse = lax.rsqrt(variance + EPSILON)
    return centred * inverse, inverse


def norm_back(grad, normal, inverse):
    return inverse * (
        grad
        - jnp.mean(grad, axis=-1, keepdims=True)
        - normal * jnp.mean(grad * normal, axis=-1, keepdims=True)
    )


def gelu_and_slope(values):
    below = 0.5 + 0.5 * lax.erf(values * (1.0 / math.sqrt(2.0)))
    bell = jnp.exp2(values * values * (-0.5 * LOG2_E))
    return values * below, below + values * bell * (1.0 / math.sqrt(2.0 * math.pi))


def segment_codes(lengths_ref, start_near, start_far, rows):
    row = lax.broadcasted_iota(jnp.int32, (rows, LANES), 0)
    half = rows // 2
    place = jnp.where(row < half, start_near + row, start_far + row - half)
    segment = jnp.zeros_like(place)
    end = jnp.int32(0)
    for pair in range(lengths_ref.shape[1]):
        end = end + lengths_ref[0, pair]
        segment = segment + (place >= end).astype(jnp.int32)
    return segment


def crosses_widely(lengths_ref, middle, half):
    end = jnp.int32(0)
    left = jnp.int32(middle)
    right = jnp.int32(middle)
    for pair in range(lengths_ref.shape[1]):
        end = end + lengths_ref[0, pair]
        left = jnp.where(end < middle, middle - end, left)
        right = jnp.where(end >= middle, jnp.minimum(right, end - middle), right)
    return (right > 0) & ((left > half) | (right > half))


def in_hbm(*arrays):
    return [pltpu.with_memory_space_constraint(a, pltpu.HBM) for a in arrays]


def own_rows(side, half):
    return pl.multiple_of((1 - side) * half, half), pl.multiple_of(side * half, half)


def project_kernel(
    x_hbm,
    wq_hbm,
    wk_hbm,
    wv_hbm,
    aqt_hbm,
    bq_hbm,
    avt_hbm,
    bv_hbm,
    wo_hbm,
    wu_hbm,
    x_ref,
    q_ref,
    k_ref,
    v_ref,
    kt_ref,
    vt_ref,
    qlow_ref,
    vlow_ref,
    wk,
    wv,
    bq,
    avt,
    bv,
    wo,
    wu,
    wq,
    aqt,
    sems,
):
    tokens = x_hbm.shape[1]
    half = tokens // 2
    near, far = own_rows(lax.axis_index("seq"), half)
    pairs = (
        (x_hbm.at[0, pl.ds(near, half)], x_ref.at[pl.ds(0, half)]),
        (x_hbm.at[0, pl.ds(far, half)], x_ref.at[pl.ds(half, half)]),
        (wk_hbm, wk),
        (aqt_hbm, aqt),
        (bq_hbm, bq),
        (avt_hbm, avt),
        (bv_hbm, bv),
        (wq_hbm, wq),
        (wv_hbm, wv),
        (wo_hbm, wo),
        (wu_hbm.at[:, pl.ds(0, wu.shape[1])], wu),
    )
    copies = [pltpu.make_async_copy(a, b, sems.at[i]) for i, (a, b) in enumerate(pairs)]
    for copy in copies:
        copy.start()
    for copy in copies[:3]:
        copy.wait()
    x = x_ref[...]
    keys = dot(x, wk[...]).astype(BF16)
    k_ref[...] = keys
    kt_ref[...] = keys.T
    for copy in copies[3:9]:
        copy.wait()
    qlow_t = dot(aqt[...], x, NT).astype(BF16)
    vlow_t = dot(avt[...], x, NT).astype(BF16)
    qlow_ref[...] = qlow_t
    vlow_ref[...] = vlow_t
    q_ref[...] = (
        (dot(x, wq[...]) + 2.0 * dot(qlow_t, bq[...], TN)) * (LOG2_E / math.sqrt(DH))
    ).astype(BF16)
    vals = (dot(x, wv[...]) + 2.0 * dot(vlow_t, bv[...], TN)).astype(BF16)
    v_ref[...] = vals
    vt_ref[...] = vals.T
    for copy in copies[9:]:
        copy.wait()


def call_project(x, wq, wk, wv, lows, wo, wu):
    _, tokens, width = x.shape
    rank = lows[1].shape[0]
    shape = jax.ShapeDtypeStruct
    rows, columns = shape((tokens, width), BF16), shape((width, tokens), BF16)
    low = shape((rank, tokens), BF16)
    square, flat = shape((width, width), BF16), shape((rank, width), BF16)
    return pl.pallas_call(
        project_kernel,
        out_shape=(rows,) * 4
        + (columns,) * 2
        + (low,) * 2
        + (square,) * 2
        + (flat,) * 3
        + (square, shape((width, EARLY * width), BF16), square, flat),
        in_specs=[pl.BlockSpec(memory_space=pltpu.HBM)] * 10,
        out_specs=(pl.BlockSpec(memory_space=pltpu.VMEM),) * 17,
        scratch_shapes=[pltpu.SemaphoreType.DMA((11,))],
        compiler_params=pltpu.CompilerParams(vmem_limit_bytes=20 * 2**20),
        cost_estimate=pl.CostEstimate(flops=10**9, bytes_accessed=8 * 10**6, transcendentals=0),
    )(*in_hbm(x, wq, wk, wv, *lows, wo, wu))


def layer_kernel(
    lengths_ref,
    x_ref,
    q_s,
    k_s,
    v_s,
    kt_s,
    vt_s,
    qlow_ref,
    vlow_ref,
    wk,
    wv,
    bq_ref,
    avt_ref,
    bv_ref,
    wo,
    wu_early,
    other_ref,
    gain_one_hbm,
    shift_one_hbm,
    gain_two_hbm,
    shift_two_hbm,
    wu_hbm,
    wd_hbm,
    cot_hbm,
    out_hbm,
    gr_s,
    dqt_s,
    ds_s,
    dv_s,
    halo_s,
    packed_ref,
    gain_one_s,
    shift_one_s,
    gain_two_s,
    shift_two_s,
    x_s,
    wu_late,
    wd,
    cot_s,
    kh_s,
    vh_s,
    kht_s,
    vht_s,
    p_s,
    inv_s,
    ct_s,
    normal_s,
    rstd_s,
    hidden_s,
    active_s,
    slope_s,
    total_s,
    out_s,
    dot_s,
    sems,
):
    tokens, width = x_ref.shape
    half = tokens // 2
    hidden = wu_hbm.shape[1]
    rank = bq_ref.shape[0]
    heads = width // DH
    side = lax.axis_index("seq")
    near, far = own_rows(side, half)

    copies = []

    def fetch(source, target):
        copy = pltpu.make_async_copy(source, target, sems.at[len(copies)])
        copies.append(copy)
        copy.start()
        return copy

    get_gains = [
        fetch(gain_one_hbm, gain_one_s),
        fetch(shift_one_hbm, shift_one_s),
        fetch(gain_two_hbm, gain_two_s),
        fetch(shift_two_hbm, shift_two_s),
    ]
    chunks = hidden // width
    early = wu_early.shape[1]
    get_ffn = [fetch(wu_hbm.at[:, pl.ds(early, hidden - early)], wu_late)]
    for c in range(chunks):
        part = pl.ds(c * width, width)
        get_ffn.append(fetch(wd_hbm.at[part], wd.at[part]))

    def wu_part(c):
        start = c * width
        if start < early:
            return wu_early[:, pl.ds(start, width)]
        return wu_late[:, pl.ds(start - early, width)]

    get_cot = [
        fetch(cot_hbm.at[0, pl.ds(near, half)], cot_s.at[pl.ds(0, half)]),
        fetch(cot_hbm.at[0, pl.ds(far, half)], cot_s.at[pl.ds(half, half)]),
    ]

    wide = crosses_widely(lengths_ref, tokens, half)
    own_segment = segment_codes(lengths_ref, side * tokens + near, side * tokens + far, tokens)
    halo_base = (1 - side) * tokens
    halo_segment = segment_codes(lengths_ref, halo_base + far, halo_base + near, tokens)
    lane = lax.broadcasted_iota(jnp.int32, (tokens, LANES), 1)
    code = lane & (DH - 1)
    low_lanes = lax.broadcasted_iota(jnp.int32, (2 * tokens, LANES), 1) < DH
    marks = lengths_ref.shape[1] + 1
    q_code = jnp.where(code == own_segment, 1.0, 0.0).astype(BF16)

    def key_code(segment):
        return jnp.where((code < marks) & (code != segment), FAR_AWAY, 0.0).astype(BF16)

    ko_code = key_code(own_segment)
    kh_code = key_code(halo_segment)

    bq, avt, bv = bq_ref[...], avt_ref[...], bv_ref[...]
    qlow_t, vlow_t = qlow_ref[...], vlow_ref[...]
    x_s[pl.ds(0, half)] = other_ref[0, pl.ds(far, half)]
    x_s[pl.ds(half, half)] = other_ref[0, pl.ds(near, half)]
    halo_low_t = dot(avt, x_s[...], NT).astype(BF16)

    def project_halo(start):
        rows = pl.ds(start, half)
        x_halo = x_s[rows]
        keys = dot(x_halo, wk[...]).astype(BF16)
        kh_s[rows] = keys
        kht_s[:, rows] = keys.T
        low_t = halo_low_t[:, start : start + half]
        vals = (dot(x_halo, wv[...]) + 2.0 * dot(low_t, bv, TN)).astype(BF16)
        vh_s[rows] = vals
        vht_s[:, rows] = vals.T

    def joined(own, halo, reach, join):
        if reach == tokens:
            return join(own, halo)
        return jnp.concatenate([join(own[:, :reach], halo), own[:, reach:]], axis=1)

    def padded(halo, reach):
        if reach == tokens:
            return halo
        return jnp.concatenate([halo, jnp.zeros((reach, tokens - reach), halo.dtype)], axis=1)

    def lanes_of(pair):
        return pl.ds(pl.multiple_of(pair * LANES, LANES), LANES)

    def rows_of(pair, odd):
        return pl.ds(pl.multiple_of(pair * LANES + odd * DH, DH), DH)

    def score(pair, odd, reach):
        lanes = lanes_of(pair)

        def mixed(values, codes):
            mask = low_lanes[: values.shape[0]]
            if odd:
                return jnp.where(mask, codes, values)
            return jnp.where(mask, values, codes)

        k_pair = jnp.concatenate([k_s[:, lanes], kh_s[pl.ds(0, reach), lanes]], axis=0)
        k_code = jnp.concatenate([ko_code, kh_code[:reach]], axis=0)
        return dot(mixed(k_pair, k_code), mixed(q_s[:, lanes], q_code), NT)

    def soften(pair, odd, reach, scores):
        head = 2 * pair + odd
        own, halo = scores[:tokens], scores[tokens:, :reach]
        peak = joined(
            jnp.max(own, axis=0, keepdims=True),
            jnp.max(halo, axis=0, keepdims=True),
            reach,
            jnp.maximum,
        )
        own = jnp.exp2(own - peak)
        halo = jnp.exp2(halo - peak[:, :reach])
        inverse = 1.0 / joined(
            jnp.sum(own, axis=0, keepdims=True),
            jnp.sum(halo, axis=0, keepdims=True),
            reach,
            jnp.add,
        )
        own, halo = own.astype(BF16), padded(halo.astype(BF16), reach)
        p_s[head, pl.ds(0, tokens)] = own
        p_s[head, pl.ds(tokens, reach)] = halo
        inv_s[head] = jnp.broadcast_to(inverse, inv_s.shape[1:])
        return own, halo, inverse

    def attend(pair, odd, reach, soft):
        own, halo, inverse = soft
        rows = rows_of(pair, odd)
        context = dot(vt_s[rows, :], own) + dot(vht_s[rows, pl.ds(0, reach)], halo)
        ct_s[rows, :] = (context * inverse).astype(BF16)

    def back_score(pair, odd, reach):
        lanes = lanes_of(pair)
        inverse = inv_s[2 * pair + odd, pl.ds(0, 1), :]
        grad = (dot_s[rows_of(pair, odd), :] * inverse).astype(BF16)
        blank = jnp.zeros_like(grad)
        grad = jnp.concatenate([blank, grad] if odd else [grad, blank], axis=0)
        own = dot(v_s[:, lanes], grad)
        halo = dot(vh_s[pl.ds(0, reach), lanes], grad[:, :reach])
        return inverse, grad, own, halo

    evens = {}

    def back_soften(pair, odd, reach, slopes):
        head = 2 * pair + odd
        inverse, grad, own, halo = slopes
        p_own, p_halo = p_s[head, pl.ds(0, tokens)], p_s[head, pl.ds(tokens, reach), pl.ds(0, reach)]
        po, ph = p_own.astype(F32), p_halo.astype(F32)
        own, halo = po * own, ph * halo
        inner = inverse * joined(
            jnp.sum(own, axis=0, keepdims=True),
            jnp.sum(halo, axis=0, keepdims=True),
            reach,
            jnp.add,
        )
        own = (own - po * inner).astype(BF16)
        halo = (halo - ph * inner[:, :reach]).astype(BF16)
        ds_s[head, pl.ds(0, tokens)] = own
        ds_s[head, pl.ds(tokens, reach), pl.ds(0, reach)] = halo
        return grad, p_own, p_halo, own, halo

    def attend_back(pair, odd, reach, soft):
        lanes, rows = lanes_of(pair), rows_of(pair, odd)
        grad, p_own, p_halo, own, halo = soft
        parts = (dot(p_own, grad, NT), dot(p_halo, grad[:, :reach], NT))
        dq = joined(
            dot(kt_s[rows, :], own),
            dot(kht_s[rows, pl.ds(0, reach)], halo),
            reach,
            jnp.add,
        )
        dqt_s[rows, :] = (dq * (1.0 / math.sqrt(DH))).astype(BF16)
        if not odd:
            evens[0] = parts
            return
        even = evens.pop(0)
        dv_s[:, lanes] = (even[0] + parts[0]).astype(BF16)
        halo_s[pl.ds(0, reach), lanes] = (even[1] + parts[1]).astype(BF16)

    def for_heads(reach, first, second, third, lags):
        if reach == tokens:

            def step(pair, none):
                for odd in range(2):
                    soft = second(pair, odd, tokens, first(pair, odd, tokens))
                    third(pair, odd, tokens, soft)

            lax.fori_loop(0, heads // 2, step, None)
            return
        todo = [(pair, odd) for pair in range(heads // 2) for odd in range(2)]
        one, two = {}, {}
        for at in range(len(todo) + lags[1]):
            if at < len(todo):
                one[at] = first(*todo[at], reach)
            back = at - lags[0]
            if 0 <= back < len(todo):
                two[back] = second(*todo[back], reach, one.pop(back))
            back = at - lags[1]
            if 0 <= back:
                third(*todo[back], reach, two.pop(back))

    def run(reach):
        project_halo(0)
        if reach == tokens:
            project_halo(half)
        for_heads(reach, score, soften, attend, (2, 4))

        for copy in get_gains:
            copy.wait()
        resid_one = x_ref[...].astype(F32) + dot(ct_s[...], wo[...], TN)
        normal, inverse = normed(resid_one)
        normal_s[...] = normal
        rstd_s[...] = jnp.broadcast_to(inverse, rstd_s.shape)
        gain_one, shift_one = gain_one_s[...].reshape(1, width), shift_one_s[...].reshape(1, width)
        gain_two, shift_two = gain_two_s[...].reshape(1, width), shift_two_s[...].reshape(1, width)
        hidden_one = normal * gain_one + shift_one
        hidden_s[...] = hidden_one.astype(BF16)
        total_s[...] = hidden_one
        for copy in get_ffn:
            copy.wait()
        upward = dot(hidden_s[...], wu_part(0))
        for c in range(chunks):
            part = pl.ds(c * width, width)
            ahead = dot(hidden_s[...], wu_part(c + 1)) if c + 1 < chunks else None
            value, slope = gelu_and_slope(upward)
            active_s[:, part] = value.astype(BF16)
            slope_s[:, part] = slope.astype(BF16)
            total_s[...] += dot(active_s[:, part], wd[part, :])
            upward = ahead
        normal_two, inverse_two = normed(total_s[...])
        out_s[...] = (normal_two * gain_two + shift_two).astype(BF16)

        def put(source, target):
            return fetch(source, target)

        puts = [
            put(out_s.at[pl.ds(0, half)], out_hbm.at[0, pl.ds(near, half)]),
            put(out_s.at[pl.ds(half, half)], out_hbm.at[0, pl.ds(far, half)]),
        ]
        for copy in get_cot:
            copy.wait()
        grad_out = cot_s[...].astype(F32)
        grad_gain_two = jnp.sum(grad_out * normal_two, axis=0, keepdims=True)
        grad_shift_two = jnp.sum(grad_out, axis=0, keepdims=True)
        grad_two = norm_back(grad_out * gain_two, normal_two, inverse_two)
        hidden_s[...] = grad_two.astype(BF16)
        total_s[...] = grad_two
        grad_active = dot(hidden_s[...], wd[pl.ds(0, width), :], NT)
        for c in range(chunks):
            part = pl.ds(c * width, width)
            ahead = None
            if c + 1 < chunks:
                ahead = dot(hidden_s[...], wd[pl.ds((c + 1) * width, width), :], NT)
            active_s[:, part] = (slope_s[:, part].astype(F32) * grad_active).astype(BF16)
            total_s[...] += dot(active_s[:, part], wu_part(c), NT)
            grad_active = ahead
        grad_hidden = total_s[...]
        normal = normal_s[...]
        grad_gain_one = jnp.sum(grad_hidden * normal, axis=0, keepdims=True)
        grad_shift_one = jnp.sum(grad_hidden, axis=0, keepdims=True)
        grad_one = norm_back(grad_hidden * gain_one, normal, rstd_s[:, :1])
        gr_s[...] = grad_one
        dot_s[...] = dot(wo[...], grad_one.astype(BF16), NT)

        if reach < tokens:
            halo_s[pl.ds(half, half)] = jnp.zeros((half, width), BF16)

        for_heads(reach, back_score, back_soften, attend_back, (2, 4))

        dv_halo = halo_s[...]
        x_own = x_ref[...]
        grad_qlow_t = (2.0 * dot(bq, dqt_s[...])).astype(BF16)
        grad_vlow_t = (2.0 * dot(bv, dv_s[...], NT)).astype(BF16)
        grad_halo_t = (2.0 * dot(bv, dv_halo, NT)).astype(BF16)
        rows = [
            dot(grad_qlow_t, x_own),
            2.0 * dot(qlow_t, dqt_s[...], NT),
            dot(grad_vlow_t, x_own) + dot(grad_halo_t, x_s[...]),
            2.0 * (dot(vlow_t, dv_s[...]) + dot(halo_low_t, dv_halo)),
            grad_gain_one,
            grad_shift_one,
            grad_gain_two,
            grad_shift_two,
        ]
        spare = packed_ref.shape[0] - 4 * rank - 4
        rows.append(jnp.zeros((spare, width), F32))
        packed_ref[...] = jnp.concatenate(rows, axis=0).astype(BF16)
        for copy in puts:
            copy.wait()

    @pl.when(jnp.logical_not(wide))
    def _():
        run(half)

    @pl.when(wide)
    def _():
        run(tokens)


def call_layer(lengths, projected, other, gains, wu, wd, cotangent):
    _, tokens, width = other.shape
    hidden = wu.shape[1]
    heads = width // DH
    rank = projected[6].shape[0]
    packed_rows = -(-(4 * rank + 4) // 8) * 8
    hbm = pl.BlockSpec(memory_space=pltpu.HBM)
    here = pl.BlockSpec(memory_space=pltpu.VMEM)
    shape = jax.ShapeDtypeStruct
    vmem = pltpu.VMEM
    return pl.pallas_call(
        layer_kernel,
        out_shape=(
            shape((1, tokens, width), BF16),
            shape((tokens, width), F32),
            shape((width, tokens), BF16),
            shape((heads, 2 * tokens, tokens), BF16),
            shape((tokens, width), BF16),
            shape((tokens, width), BF16),
            shape((packed_rows, width), BF16),
        ),
        in_specs=[pl.BlockSpec(memory_space=pltpu.SMEM)] + [here] * 16 + [hbm] * 7,
        out_specs=(hbm,) + (here,) * 6,
        scratch_shapes=[
            vmem((width,), F32),
            vmem((width,), F32),
            vmem((width,), F32),
            vmem((width,), F32),
            vmem((tokens, width), BF16),
            vmem((width, hidden - EARLY * width), BF16),
            vmem(wd.shape, BF16),
            vmem((tokens, width), BF16),
            vmem((tokens, width), BF16),
            vmem((tokens, width), BF16),
            vmem((width, tokens), BF16),
            vmem((width, tokens), BF16),
            vmem((heads, 2 * tokens, tokens), BF16),
            vmem((heads, 8, tokens), F32),
            vmem((width, tokens), BF16),
            vmem((tokens, width), F32),
            vmem((tokens, LANES), F32),
            vmem((tokens, width), BF16),
            vmem((tokens, hidden), BF16),
            vmem((tokens, hidden), BF16),
            vmem((tokens, width), F32),
            vmem((tokens, width), BF16),
            vmem((width, tokens), F32),
            pltpu.SemaphoreType.DMA((32,)),
        ],
        compiler_params=pltpu.CompilerParams(vmem_limit_bytes=36 * 2**20),
        cost_estimate=pl.CostEstimate(flops=9 * 10**9, bytes_accessed=15 * 10**6, transcendentals=0),
    )(lengths, *projected, other, *in_hbm(*gains, wu, wd, cotangent))


def keys_kernel(
    lengths_ref,
    q_ref,
    ds_ref,
    dv_ref,
    wk,
    wv,
    avt,
    bv,
    dk_ref,
    sent_ref,
    halo_s,
):
    tokens, width = q_ref.shape
    half = tokens // 2
    wide = crosses_widely(lengths_ref, tokens, half)
    low_lanes = lax.broadcasted_iota(jnp.int32, (tokens, LANES), 1) < DH
    unscale = 1.0 / LOG2_E

    def step(pair, reach):
        lanes = pl.ds(pl.multiple_of(pair * LANES, LANES), LANES)
        q_pair = q_ref[:, lanes]
        own = [dot(ds_ref[2 * pair + odd, pl.ds(0, tokens)], q_pair) for odd in range(2)]
        halo = [
            dot(ds_ref[2 * pair + odd, pl.ds(tokens, reach), pl.ds(0, reach)], q_pair[:reach])
            for odd in range(2)
        ]
        dk_ref[:, lanes] = (jnp.where(low_lanes, *own) * unscale).astype(BF16)
        halo_s[pl.ds(0, reach), lanes] = (
            jnp.where(low_lanes[:reach], *halo) * unscale
        ).astype(BF16)

    def send(reach):
        rows = pl.ds(0, reach)
        grad_v = dv_ref[rows]
        low_t = (2.0 * dot(bv[...], grad_v, NT)).astype(BF16)
        sent_ref[rows] = (
            dot(halo_s[rows], wk[...], NT) + dot(grad_v, wv[...], NT) + dot(low_t, avt[...], TN)
        ).astype(BF16)

    @pl.when(jnp.logical_not(wide))
    def _():
        for pair in range(width // LANES):
            step(pair, half)

    @pl.when(wide)
    def _():
        lax.fori_loop(0, width // LANES, lambda pair, none: step(pair, tokens), None)

    @pl.when(jnp.logical_not(wide))
    def _():
        sent_ref[pl.ds(half, half)] = jnp.zeros((half, width), BF16)
        send(half)

    @pl.when(wide)
    def _():
        send(tokens)


def call_keys(lengths, q, ds, dv_halo, wk, wv, avt, bv):
    tokens, width = q.shape
    rows = jax.ShapeDtypeStruct((tokens, width), BF16)
    return pl.pallas_call(
        keys_kernel,
        out_shape=(rows, rows),
        in_specs=[pl.BlockSpec(memory_space=pltpu.SMEM)]
        + [pl.BlockSpec(memory_space=pltpu.VMEM)] * 7,
        out_specs=(pl.BlockSpec(memory_space=pltpu.VMEM),) * 2,
        scratch_shapes=[pltpu.VMEM((tokens, width), BF16)],
        compiler_params=pltpu.CompilerParams(vmem_limit_bytes=6 * 2**20),
        cost_estimate=pl.CostEstimate(flops=2 * 10**9, bytes_accessed=6 * 10**6, transcendentals=0),
    )(lengths, q, ds, dv_halo, wk, wv, avt, bv)


def inputs_kernel(
    received_ref,
    gr,
    dqt,
    dk,
    dv,
    wq,
    wk,
    wv,
    aqt,
    bq,
    avt,
    bv,
    out_hbm,
    out_s,
    sems,
):
    tokens, width = gr.shape
    half = tokens // 2
    near, far = own_rows(lax.axis_index("seq"), half)
    grad_qlow_t = (2.0 * dot(bq[...], dqt[...])).astype(BF16)
    grad_vlow_t = (2.0 * dot(bv[...], dv[...], NT)).astype(BF16)
    out_s[...] = (
        gr[...]
        + received_ref[...].astype(F32)
        + dot(dk[...], wk[...], NT)
        + dot(dv[...], wv[...], NT)
        + dot(dqt[...], wq[...], TT)
        + dot(grad_qlow_t, aqt[...], TN)
        + dot(grad_vlow_t, avt[...], TN)
    )
    puts = [
        pltpu.make_async_copy(
            out_s.at[pl.ds(0, half)], out_hbm.at[0, pl.ds(near, half)], sems.at[0]
        ),
        pltpu.make_async_copy(
            out_s.at[pl.ds(half, half)], out_hbm.at[0, pl.ds(far, half)], sems.at[1]
        ),
    ]
    for copy in puts:
        copy.start()
    for copy in puts:
        copy.wait()


def call_inputs(received, gr, dqt, dk, dv, *weights):
    tokens, width = gr.shape
    return pl.pallas_call(
        inputs_kernel,
        out_shape=jax.ShapeDtypeStruct((1, tokens, width), F32),
        in_specs=[pl.BlockSpec(memory_space=pltpu.VMEM)] * 12,
        out_specs=pl.BlockSpec(memory_space=pltpu.HBM),
        scratch_shapes=[pltpu.VMEM((tokens, width), F32), pltpu.SemaphoreType.DMA((2,))],
        compiler_params=pltpu.CompilerParams(vmem_limit_bytes=6 * 2**20),
        cost_estimate=pl.CostEstimate(flops=2 * 10**9, bytes_accessed=6 * 10**6, transcendentals=0),
    )(received, gr, dqt, dk, dv, *weights)


def finish_kernel(rank, count, *refs):
    ins, outs = refs[:count], refs[count : count + 8]
    scratch, singles, sems = refs[-6], refs[-5:-1], refs[-1]
    total = ins[0][...].astype(F32)
    for one in ins[1:]:
        total = total + one[...].astype(F32)
    scratch[...] = total
    copies = []
    for i, out in enumerate(outs):
        if i < 4:
            source = scratch.at[pl.ds(i * rank, rank)]
        else:
            source = singles[i - 4]
            source[...] = total[4 * rank + i - 4]
        copies.append(pltpu.make_async_copy(source, out, sems.at[i]))
    for copy in copies:
        copy.start()
    for copy in copies:
        copy.wait()


def call_finish(rank, parts):
    rows, width = parts[0].shape
    shape = jax.ShapeDtypeStruct
    return pl.pallas_call(
        functools.partial(finish_kernel, rank, len(parts)),
        out_shape=(shape((rank, width), F32),) * 4 + (shape((width,), F32),) * 4,
        in_specs=[pl.BlockSpec(memory_space=pltpu.VMEM)] * len(parts),
        out_specs=(pl.BlockSpec(memory_space=pltpu.HBM),) * 8,
        scratch_shapes=[pltpu.VMEM((rows, width), F32)]
        + [pltpu.VMEM((width,), F32)] * 4
        + [pltpu.SemaphoreType.DMA((8,))],
        compiler_params=pltpu.CompilerParams(vmem_limit_bytes=4 * 2**20),
    )(*parts)


def swapped(values, axis, partners):
    size = lax.axis_size(axis)
    return [values] + [
        lax.ppermute(values, axis, [(i, i ^ p) for i in range(size)]) for p in partners
    ]


def added(parts):
    total = parts[0].astype(F32)
    for one in parts[1:]:
        total = total + one.astype(F32)
    return total.astype(BF16)


def parts_of_sum(values, beside):
    parts = swapped(values, "seq", (1,))
    stride, size = 1, lax.axis_size("dp")
    while stride < size:
        radix = min(4, size // stride)
        parts = swapped(added(parts), "dp", [stride * k for k in range(1, radix)])
        if stride == 1:
            *parts, beside = lax.optimization_barrier((*parts, beside))
        stride *= radix
    return parts, beside


def body(
    inputs,
    pair_lengths,
    w_query,
    w_key,
    w_value,
    w_out,
    w_up,
    w_down,
    a_query,
    b_query,
    a_value,
    b_value,
    gain_one,
    shift_one,
    gain_two,
    shift_two,
    cotangent,
):
    rank = a_query.shape[1]
    swap = [(0, 1), (1, 0)]
    other = lax.ppermute(inputs, "seq", swap)
    lows = (a_query.T, b_query, a_value.T, b_value)
    gains = (gain_one, shift_one, gain_two, shift_two)
    *projected, wq, aqt = call_project(inputs, w_query, w_key, w_value, lows, w_out, w_up)
    wk, wv, bq, avt, bv = projected[8:13]
    output, gr, dqt, ds, dv, dv_halo, packed = call_layer(
        pair_lengths, projected, other, gains, w_up, w_down, cotangent
    )
    beside = call_keys(pair_lengths, projected[1], ds, dv_halo, wk, wv, avt, bv)
    parts, (dk, sent) = parts_of_sum(packed, beside)
    received = lax.ppermute(sent, "seq", swap)
    grad_inputs = call_inputs(received, gr, dqt, dk, dv, wq, wk, wv, aqt, bq, avt, bv)
    *parts, grad_inputs = lax.optimization_barrier((*parts, grad_inputs))
    gaq, gbq, gav, gbv, *norms = call_finish(rank, parts)
    return (output, grad_inputs, gaq.T, gbq, gav.T, gbv, *norms)


def solution(mesh):
    tokens = P("dp", "seq", None)
    in_specs = (tokens, P("dp", None)) + (P(),) * 14 + (tokens,)
    out_specs = (tokens, tokens) + (P(),) * 8
    return jax.shard_map(body, mesh=mesh, in_specs=in_specs, out_specs=out_specs, check_vma=False)
```

```python
import functools
import math

import jax
import jax.numpy as jnp
from jax import lax
from jax.experimental import pallas as pl
from jax.experimental.pallas import tpu as pltpu
from jax.sharding import PartitionSpec as P

DH = 64
LANES = 128
EARLY = 3
EPSILON = 1e-05
LOG2_E = math.log2(math.e)
FAR_AWAY = -1e30
BF16 = jnp.bfloat16
F32 = jnp.float32
NN = ((1,), (0,))
NT = ((1,), (1,))
TN = ((0,), (0,))
TT = ((0,), (1,))


def dot(former, latter, dims=NN):
    return lax.dot_general(former, latter, (dims, ((), ())), preferred_element_type=F32)


def normed(values):
    centred = values - jnp.mean(values, axis=-1, keepdims=True)
    variance = jnp.mean(centred * centred, axis=-1, keepdims=True)
    inverse = lax.rsqrt(variance + EPSILON)
    return centred * inverse, inverse


def norm_back(grad, normal, inverse):
    return inverse * (
        grad
        - jnp.mean(grad, axis=-1, keepdims=True)
        - normal * jnp.mean(grad * normal, axis=-1, keepdims=True)
    )


def gelu_and_slope(values):
    below = 0.5 + 0.5 * lax.erf(values * (1.0 / math.sqrt(2.0)))
    bell = jnp.exp2(values * values * (-0.5 * LOG2_E))
    return values * below, below + values * bell * (1.0 / math.sqrt(2.0 * math.pi))


def segment_codes(lengths_ref, start_near, start_far, rows):
    row = lax.broadcasted_iota(jnp.int32, (rows, LANES), 0)
    half = rows // 2
    place = jnp.where(row < half, start_near + row, start_far + row - half)
    segment = jnp.zeros_like(place)
    end = jnp.int32(0)
    for pair in range(lengths_ref.shape[1]):
        end = end + lengths_ref[0, pair]
        segment = segment + (place >= end).astype(jnp.int32)
    return segment


def crosses_widely(lengths_ref, middle, half):
    end = jnp.int32(0)
    left = jnp.int32(middle)
    right = jnp.int32(middle)
    for pair in range(lengths_ref.shape[1]):
        end = end + lengths_ref[0, pair]
        left = jnp.where(end < middle, middle - end, left)
        right = jnp.where(end >= middle, jnp.minimum(right, end - middle), right)
    return (right > 0) & ((left > half) | (right > half))


def in_hbm(*arrays):
    return [pltpu.with_memory_space_constraint(a, pltpu.HBM) for a in arrays]


def own_rows(side, half):
    return pl.multiple_of((1 - side) * half, half), pl.multiple_of(side * half, half)


def project_kernel(
    x_hbm,
    wq_hbm,
    wk_hbm,
    wv_hbm,
    aqt_hbm,
    bq_hbm,
    avt_hbm,
    bv_hbm,
    wo_hbm,
    wu_hbm,
    x_ref,
    q_ref,
    k_ref,
    v_ref,
    kt_ref,
    vt_ref,
    qlow_ref,
    vlow_ref,
    wk,
    wv,
    bq,
    avt,
    bv,
    wo,
    wu,
    wq,
    aqt,
    sems,
):
    tokens = x_hbm.shape[1]
    half = tokens // 2
    near, far = own_rows(lax.axis_index("seq"), half)
    pairs = (
        (x_hbm.at[0, pl.ds(near, half)], x_ref.at[pl.ds(0, half)]),
        (x_hbm.at[0, pl.ds(far, half)], x_ref.at[pl.ds(half, half)]),
        (wk_hbm, wk),
        (aqt_hbm, aqt),
        (bq_hbm, bq),
        (avt_hbm, avt),
        (bv_hbm, bv),
        (wq_hbm, wq),
        (wv_hbm, wv),
        (wo_hbm, wo),
        (wu_hbm.at[:, pl.ds(0, wu.shape[1])], wu),
    )
    copies = [pltpu.make_async_copy(a, b, sems.at[i]) for i, (a, b) in enumerate(pairs)]
    for copy in copies:
        copy.start()
    for copy in copies[:3]:
        copy.wait()
    x = x_ref[...]
    keys = dot(x, wk[...]).astype(BF16)
    k_ref[...] = keys
    kt_ref[...] = keys.T
    for copy in copies[3:9]:
        copy.wait()
    qlow_t = dot(aqt[...], x, NT).astype(BF16)
    vlow_t = dot(avt[...], x, NT).astype(BF16)
    qlow_ref[...] = qlow_t
    vlow_ref[...] = vlow_t
    vals = (dot(x, wv[...]) + 2.0 * dot(vlow_t, bv[...], TN)).astype(BF16)
    v_ref[...] = vals
    vt_ref[...] = vals.T
    q_ref[...] = (
        (dot(x, wq[...]) + 2.0 * dot(qlow_t, bq[...], TN)) * (LOG2_E / math.sqrt(DH))
    ).astype(BF16)
    for copy in copies[9:]:
        copy.wait()


def call_project(x, wq, wk, wv, lows, wo, wu):
    _, tokens, width = x.shape
    rank = lows[1].shape[0]
    shape = jax.ShapeDtypeStruct
    rows, columns = shape((tokens, width), BF16), shape((width, tokens), BF16)
    low = shape((rank, tokens), BF16)
    square, flat = shape((width, width), BF16), shape((rank, width), BF16)
    return pl.pallas_call(
        project_kernel,
        out_shape=(rows,) * 4
        + (columns,) * 2
        + (low,) * 2
        + (square,) * 2
        + (flat,) * 3
        + (square, shape((width, EARLY * width), BF16), square, flat),
        in_specs=[pl.BlockSpec(memory_space=pltpu.HBM)] * 10,
        out_specs=(pl.BlockSpec(memory_space=pltpu.VMEM),) * 17,
        scratch_shapes=[pltpu.SemaphoreType.DMA((11,))],
        compiler_params=pltpu.CompilerParams(vmem_limit_bytes=20 * 2**20),
        cost_estimate=pl.CostEstimate(flops=10**9, bytes_accessed=8 * 10**6, transcendentals=0),
    )(*in_hbm(x, wq, wk, wv, *lows, wo, wu))


def layer_kernel(
    lengths_ref,
    x_ref,
    q_s,
    k_s,
    v_s,
    kt_s,
    vt_s,
    qlow_ref,
    vlow_ref,
    wk,
    wv,
    bq_ref,
    avt_ref,
    bv_ref,
    wo,
    wu_early,
    other_ref,
    gain_one_hbm,
    shift_one_hbm,
    gain_two_hbm,
    shift_two_hbm,
    wu_hbm,
    wd_hbm,
    cot_hbm,
    out_hbm,
    gr_s,
    dqt_s,
    ds_s,
    dv_s,
    halo_s,
    packed_ref,
    gain_one_s,
    shift_one_s,
    gain_two_s,
    shift_two_s,
    x_s,
    wu_late,
    wd,
    cot_s,
    kh_s,
    vh_s,
    kht_s,
    vht_s,
    p_s,
    inv_s,
    ct_s,
    normal_s,
    rstd_s,
    hidden_s,
    active_s,
    slope_s,
    total_s,
    out_s,
    dot_s,
    sems,
):
    tokens, width = x_ref.shape
    half = tokens // 2
    hidden = wu_hbm.shape[1]
    rank = bq_ref.shape[0]
    heads = width // DH
    side = lax.axis_index("seq")
    near, far = own_rows(side, half)

    copies = []

    def fetch(source, target):
        copy = pltpu.make_async_copy(source, target, sems.at[len(copies)])
        copies.append(copy)
        copy.start()
        return copy

    get_gains = [
        fetch(gain_one_hbm, gain_one_s),
        fetch(shift_one_hbm, shift_one_s),
        fetch(gain_two_hbm, gain_two_s),
        fetch(shift_two_hbm, shift_two_s),
    ]
    chunks = hidden // width
    early = wu_early.shape[1]
    get_ffn = [fetch(wu_hbm.at[:, pl.ds(early, hidden - early)], wu_late)]
    for c in range(chunks):
        part = pl.ds(c * width, width)
        get_ffn.append(fetch(wd_hbm.at[part], wd.at[part]))

    def wu_part(c):
        start = c * width
        if start < early:
            return wu_early[:, pl.ds(start, width)]
        return wu_late[:, pl.ds(start - early, width)]

    get_cot = [
        fetch(cot_hbm.at[0, pl.ds(near, half)], cot_s.at[pl.ds(0, half)]),
        fetch(cot_hbm.at[0, pl.ds(far, half)], cot_s.at[pl.ds(half, half)]),
    ]

    wide = crosses_widely(lengths_ref, tokens, half)
    own_segment = segment_codes(lengths_ref, side * tokens + near, side * tokens + far, tokens)
    halo_base = (1 - side) * tokens
    halo_segment = segment_codes(lengths_ref, halo_base + far, halo_base + near, tokens)
    lane = lax.broadcasted_iota(jnp.int32, (tokens, LANES), 1)
    code = lane & (DH - 1)
    low_lanes = lax.broadcasted_iota(jnp.int32, (2 * tokens, LANES), 1) < DH
    marks = lengths_ref.shape[1] + 1
    q_code = jnp.where(code == own_segment, 1.0, 0.0).astype(BF16)

    def key_code(segment):
        return jnp.where((code < marks) & (code != segment), FAR_AWAY, 0.0).astype(BF16)

    ko_code = key_code(own_segment)
    kh_code = key_code(halo_segment)

    bq, avt, bv = bq_ref[...], avt_ref[...], bv_ref[...]
    qlow_t, vlow_t = qlow_ref[...], vlow_ref[...]
    x_s[pl.ds(0, half)] = other_ref[0, pl.ds(far, half)]
    x_s[pl.ds(half, half)] = other_ref[0, pl.ds(near, half)]
    halo_low_t = dot(avt, x_s[...], NT).astype(BF16)

    def project_halo(start):
        rows = pl.ds(start, half)
        x_halo = x_s[rows]
        keys = dot(x_halo, wk[...]).astype(BF16)
        kh_s[rows] = keys
        kht_s[:, rows] = keys.T
        low_t = halo_low_t[:, start : start + half]
        vals = (dot(x_halo, wv[...]) + 2.0 * dot(low_t, bv, TN)).astype(BF16)
        vh_s[rows] = vals
        vht_s[:, rows] = vals.T

    def joined(own, halo, reach, join):
        if reach == tokens:
            return join(own, halo)
        return jnp.concatenate([join(own[:, :reach], halo), own[:, reach:]], axis=1)

    def lanes_of(pair):
        return pl.ds(pl.multiple_of(pair * LANES, LANES), LANES)

    def rows_of(pair, odd):
        return pl.ds(pl.multiple_of(pair * LANES + odd * DH, DH), DH)

    def score(pair, odd, reach):
        lanes = lanes_of(pair)

        def mixed(values, codes):
            mask = low_lanes[: values.shape[0]]
            if odd:
                return jnp.where(mask, codes, values)
            return jnp.where(mask, values, codes)

        k_pair = jnp.concatenate([k_s[:, lanes], kh_s[pl.ds(0, reach), lanes]], axis=0)
        k_code = jnp.concatenate([ko_code, kh_code[:reach]], axis=0)
        return dot(mixed(k_pair, k_code), mixed(q_s[:, lanes], q_code), NT)

    def soften(pair, odd, reach, scores):
        head = 2 * pair + odd
        own, halo = scores[:tokens], scores[tokens:, :reach]
        peak = joined(
            jnp.max(own, axis=0, keepdims=True),
            jnp.max(halo, axis=0, keepdims=True),
            reach,
            jnp.maximum,
        )
        own = jnp.exp2(own - peak)
        halo = jnp.exp2(halo - peak[:, :reach])
        inverse = 1.0 / joined(
            jnp.sum(own, axis=0, keepdims=True),
            jnp.sum(halo, axis=0, keepdims=True),
            reach,
            jnp.add,
        )
        own, halo = own.astype(BF16), halo.astype(BF16)
        p_s[head, pl.ds(0, tokens)] = own
        p_s[head, pl.ds(tokens, reach), pl.ds(0, reach)] = halo
        inv_s[head] = jnp.broadcast_to(inverse, inv_s.shape[1:])
        return own, halo, inverse

    def attend(pair, odd, reach, soft):
        own, halo, inverse = soft
        rows = rows_of(pair, odd)
        context = joined(
            dot(vt_s[rows, :], own),
            dot(vht_s[rows, pl.ds(0, reach)], halo),
            reach,
            jnp.add,
        )
        ct_s[rows, :] = (context * inverse).astype(BF16)

    def back_score(pair, odd, reach):
        lanes = lanes_of(pair)
        inverse = inv_s[2 * pair + odd, pl.ds(0, 1), :]
        grad = (dot_s[rows_of(pair, odd), :] * inverse).astype(BF16)
        blank = jnp.zeros_like(grad)
        grad = jnp.concatenate([blank, grad] if odd else [grad, blank], axis=0)
        own = dot(v_s[:, lanes], grad)
        halo = dot(vh_s[pl.ds(0, reach), lanes], grad[:, :reach])
        return inverse, grad, own, halo

    evens = {}

    def back_soften(pair, odd, reach, slopes):
        head = 2 * pair + odd
        inverse, grad, own, halo = slopes
        p_own, p_halo = p_s[head, pl.ds(0, tokens)], p_s[head, pl.ds(tokens, reach), pl.ds(0, reach)]
        po, ph = p_own.astype(F32), p_halo.astype(F32)
        own, halo = po * own, ph * halo
        inner = inverse * joined(
            jnp.sum(own, axis=0, keepdims=True),
            jnp.sum(halo, axis=0, keepdims=True),
            reach,
            jnp.add,
        )
        own = (own - po * inner).astype(BF16)
        halo = (halo - ph * inner[:, :reach]).astype(BF16)
        ds_s[head, pl.ds(0, tokens)] = own
        ds_s[head, pl.ds(tokens, reach), pl.ds(0, reach)] = halo
        return grad, p_own, p_halo, own, halo

    def attend_back(pair, odd, reach, soft):
        lanes, rows = lanes_of(pair), rows_of(pair, odd)
        grad, p_own, p_halo, own, halo = soft
        parts = (dot(p_own, grad, NT), dot(p_halo, grad[:, :reach], NT))
        dq = joined(
            dot(kt_s[rows, :], own),
            dot(kht_s[rows, pl.ds(0, reach)], halo),
            reach,
            jnp.add,
        )
        dqt_s[rows, :] = (dq * (1.0 / math.sqrt(DH))).astype(BF16)
        if not odd:
            evens[0] = parts
            return
        even = evens.pop(0)
        dv_s[:, lanes] = (even[0] + parts[0]).astype(BF16)
        halo_s[pl.ds(0, reach), lanes] = (even[1] + parts[1]).astype(BF16)

    def for_heads(reach, first, second, third, lags):
        if reach == tokens:

            def step(pair, none):
                for odd in range(2):
                    soft = second(pair, odd, tokens, first(pair, odd, tokens))
                    third(pair, odd, tokens, soft)

            lax.fori_loop(0, heads // 2, step, None)
            return
        todo = [(pair, odd) for pair in range(heads // 2) for odd in range(2)]
        one, two = {}, {}
        for at in range(len(todo) + lags[1]):
            if at < len(todo):
                one[at] = first(*todo[at], reach)
            back = at - lags[0]
            if 0 <= back < len(todo):
                two[back] = second(*todo[back], reach, one.pop(back))
            back = at - lags[1]
            if 0 <= back:
                third(*todo[back], reach, two.pop(back))

    def run(reach):
        project_halo(0)
        if reach == tokens:
            project_halo(half)
        for_heads(reach, score, soften, attend, (2, 4))

        for copy in get_gains:
            copy.wait()
        resid_one = x_ref[...].astype(F32) + dot(ct_s[...], wo[...], TN)
        normal, inverse = normed(resid_one)
        normal_s[...] = normal
        rstd_s[...] = jnp.broadcast_to(inverse, rstd_s.shape)
        gain_one, shift_one = gain_one_s[...].reshape(1, width), shift_one_s[...].reshape(1, width)
        gain_two, shift_two = gain_two_s[...].reshape(1, width), shift_two_s[...].reshape(1, width)
        hidden_one = normal * gain_one + shift_one
        hidden_s[...] = hidden_one.astype(BF16)
        total_s[...] = hidden_one
        for copy in get_ffn:
            copy.wait()
        upward = dot(hidden_s[...], wu_part(0))
        for c in range(chunks):
            part = pl.ds(c * width, width)
            ahead = dot(hidden_s[...], wu_part(c + 1)) if c + 1 < chunks else None
            value, slope = gelu_and_slope(upward)
            active_s[:, part] = value.astype(BF16)
            slope_s[:, part] = slope.astype(BF16)
            total_s[...] += dot(active_s[:, part], wd[part, :])
            upward = ahead
        normal_two, inverse_two = normed(total_s[...])
        out_s[...] = (normal_two * gain_two + shift_two).astype(BF16)

        def put(source, target):
            return fetch(source, target)

        puts = [
            put(out_s.at[pl.ds(0, half)], out_hbm.at[0, pl.ds(near, half)]),
            put(out_s.at[pl.ds(half, half)], out_hbm.at[0, pl.ds(far, half)]),
        ]
        for copy in get_cot:
            copy.wait()
        grad_out = cot_s[...].astype(F32)
        grad_gain_two = jnp.sum(grad_out * normal_two, axis=0, keepdims=True)
        grad_shift_two = jnp.sum(grad_out, axis=0, keepdims=True)
        grad_two = norm_back(grad_out * gain_two, normal_two, inverse_two)
        hidden_s[...] = grad_two.astype(BF16)
        total_s[...] = grad_two
        grad_active = dot(hidden_s[...], wd[pl.ds(0, width), :], NT)
        for c in range(chunks):
            part = pl.ds(c * width, width)
            ahead = None
            if c + 1 < chunks:
                ahead = dot(hidden_s[...], wd[pl.ds((c + 1) * width, width), :], NT)
            active_s[:, part] = (slope_s[:, part].astype(F32) * grad_active).astype(BF16)
            total_s[...] += dot(active_s[:, part], wu_part(c), NT)
            grad_active = ahead
        grad_hidden = total_s[...]
        normal = normal_s[...]
        grad_gain_one = jnp.sum(grad_hidden * normal, axis=0, keepdims=True)
        grad_shift_one = jnp.sum(grad_hidden, axis=0, keepdims=True)
        grad_one = norm_back(grad_hidden * gain_one, normal, rstd_s[:, :1])
        gr_s[...] = grad_one
        dot_s[...] = dot(wo[...], grad_one.astype(BF16), NT)

        if reach < tokens:
            halo_s[pl.ds(half, half)] = jnp.zeros((half, width), BF16)

        for_heads(reach, back_score, back_soften, attend_back, (2, 4))

        dv_halo = halo_s[pl.ds(0, reach)]
        x_own = x_ref[...]
        grad_qlow_t = (2.0 * dot(bq, dqt_s[...])).astype(BF16)
        grad_vlow_t = (2.0 * dot(bv, dv_s[...], NT)).astype(BF16)
        grad_halo_t = (2.0 * dot(bv, dv_halo, NT)).astype(BF16)
        rows = [
            dot(grad_qlow_t, x_own),
            2.0 * dot(qlow_t, dqt_s[...], NT),
            dot(grad_vlow_t, x_own) + dot(grad_halo_t, x_s[pl.ds(0, reach)]),
            2.0 * (dot(vlow_t, dv_s[...]) + dot(halo_low_t[:, :reach], dv_halo)),
            grad_gain_one,
            grad_shift_one,
            grad_gain_two,
            grad_shift_two,
        ]
        spare = packed_ref.shape[0] - 4 * rank - 4
        rows.append(jnp.zeros((spare, width), F32))
        packed_ref[...] = jnp.concatenate(rows, axis=0).astype(BF16)
        for copy in puts:
            copy.wait()

    @pl.when(jnp.logical_not(wide))
    def _():
        run(half)

    @pl.when(wide)
    def _():
        run(tokens)


def call_layer(lengths, projected, other, gains, wu, wd, cotangent):
    _, tokens, width = other.shape
    hidden = wu.shape[1]
    heads = width // DH
    rank = projected[6].shape[0]
    packed_rows = -(-(4 * rank + 4) // 8) * 8
    hbm = pl.BlockSpec(memory_space=pltpu.HBM)
    here = pl.BlockSpec(memory_space=pltpu.VMEM)
    shape = jax.ShapeDtypeStruct
    vmem = pltpu.VMEM
    return pl.pallas_call(
        layer_kernel,
        out_shape=(
            shape((1, tokens, width), BF16),
            shape((tokens, width), F32),
            shape((width, tokens), BF16),
            shape((heads, 2 * tokens, tokens), BF16),
            shape((tokens, width), BF16),
            shape((tokens, width), BF16),
            shape((packed_rows, width), BF16),
        ),
        in_specs=[pl.BlockSpec(memory_space=pltpu.SMEM)] + [here] * 16 + [hbm] * 7,
        out_specs=(hbm,) + (here,) * 6,
        scratch_shapes=[
            vmem((width,), F32),
            vmem((width,), F32),
            vmem((width,), F32),
            vmem((width,), F32),
            vmem((tokens, width), BF16),
            vmem((width, hidden - EARLY * width), BF16),
            vmem(wd.shape, BF16),
            vmem((tokens, width), BF16),
            vmem((tokens, width), BF16),
            vmem((tokens, width), BF16),
            vmem((width, tokens), BF16),
            vmem((width, tokens), BF16),
            vmem((heads, 2 * tokens, tokens), BF16),
            vmem((heads, 8, tokens), F32),
            vmem((width, tokens), BF16),
            vmem((tokens, width), F32),
            vmem((tokens, LANES), F32),
            vmem((tokens, width), BF16),
            vmem((tokens, hidden), BF16),
            vmem((tokens, hidden), BF16),
            vmem((tokens, width), F32),
            vmem((tokens, width), BF16),
            vmem((width, tokens), F32),
            pltpu.SemaphoreType.DMA((32,)),
        ],
        compiler_params=pltpu.CompilerParams(vmem_limit_bytes=36 * 2**20),
        cost_estimate=pl.CostEstimate(flops=9 * 10**9, bytes_accessed=15 * 10**6, transcendentals=0),
    )(lengths, *projected, other, *in_hbm(*gains, wu, wd, cotangent))


def keys_kernel(
    lengths_ref,
    q_ref,
    ds_ref,
    dv_ref,
    wk,
    wv,
    avt,
    bv,
    dk_ref,
    sent_ref,
    halo_s,
):
    tokens, width = q_ref.shape
    half = tokens // 2
    wide = crosses_widely(lengths_ref, tokens, half)
    low_lanes = lax.broadcasted_iota(jnp.int32, (tokens, LANES), 1) < DH
    unscale = 1.0 / LOG2_E

    def step(pair, reach):
        lanes = pl.ds(pl.multiple_of(pair * LANES, LANES), LANES)
        q_pair = q_ref[:, lanes]
        own = [dot(ds_ref[2 * pair + odd, pl.ds(0, tokens)], q_pair) for odd in range(2)]
        halo = [
            dot(ds_ref[2 * pair + odd, pl.ds(tokens, reach), pl.ds(0, reach)], q_pair[:reach])
            for odd in range(2)
        ]
        dk_ref[:, lanes] = (jnp.where(low_lanes, *own) * unscale).astype(BF16)
        halo_s[pl.ds(0, reach), lanes] = (
            jnp.where(low_lanes[:reach], *halo) * unscale
        ).astype(BF16)

    def send(reach):
        rows = pl.ds(0, reach)
        grad_v = dv_ref[rows]
        low_t = (2.0 * dot(bv[...], grad_v, NT)).astype(BF16)
        sent_ref[rows] = (
            dot(halo_s[rows], wk[...], NT) + dot(grad_v, wv[...], NT) + dot(low_t, avt[...], TN)
        ).astype(BF16)

    @pl.when(jnp.logical_not(wide))
    def _():
        for pair in range(width // LANES):
            step(pair, half)

    @pl.when(wide)
    def _():
        lax.fori_loop(0, width // LANES, lambda pair, none: step(pair, tokens), None)

    @pl.when(jnp.logical_not(wide))
    def _():
        sent_ref[pl.ds(half, half)] = jnp.zeros((half, width), BF16)
        send(half)

    @pl.when(wide)
    def _():
        send(tokens)


def call_keys(lengths, q, ds, dv_halo, wk, wv, avt, bv):
    tokens, width = q.shape
    rows = jax.ShapeDtypeStruct((tokens, width), BF16)
    return pl.pallas_call(
        keys_kernel,
        out_shape=(rows, rows),
        in_specs=[pl.BlockSpec(memory_space=pltpu.SMEM)]
        + [pl.BlockSpec(memory_space=pltpu.VMEM)] * 7,
        out_specs=(pl.BlockSpec(memory_space=pltpu.VMEM),) * 2,
        scratch_shapes=[pltpu.VMEM((tokens, width), BF16)],
        compiler_params=pltpu.CompilerParams(vmem_limit_bytes=6 * 2**20),
        cost_estimate=pl.CostEstimate(flops=2 * 10**9, bytes_accessed=6 * 10**6, transcendentals=0),
    )(lengths, q, ds, dv_halo, wk, wv, avt, bv)


def inputs_kernel(
    received_ref,
    gr,
    dqt,
    dk,
    dv,
    wq,
    wk,
    wv,
    aqt,
    bq,
    avt,
    bv,
    out_hbm,
    out_s,
    sems,
):
    tokens, width = gr.shape
    half = tokens // 2
    near, far = own_rows(lax.axis_index("seq"), half)
    grad_qlow_t = (2.0 * dot(bq[...], dqt[...])).astype(BF16)
    grad_vlow_t = (2.0 * dot(bv[...], dv[...], NT)).astype(BF16)
    out_s[...] = (
        gr[...]
        + received_ref[...].astype(F32)
        + dot(dk[...], wk[...], NT)
        + dot(dv[...], wv[...], NT)
        + dot(dqt[...], wq[...], TT)
        + dot(grad_qlow_t, aqt[...], TN)
        + dot(grad_vlow_t, avt[...], TN)
    )
    puts = [
        pltpu.make_async_copy(
            out_s.at[pl.ds(0, half)], out_hbm.at[0, pl.ds(near, half)], sems.at[0]
        ),
        pltpu.make_async_copy(
            out_s.at[pl.ds(half, half)], out_hbm.at[0, pl.ds(far, half)], sems.at[1]
        ),
    ]
    for copy in puts:
        copy.start()
    for copy in puts:
        copy.wait()


def call_inputs(received, gr, dqt, dk, dv, *weights):
    tokens, width = gr.shape
    return pl.pallas_call(
        inputs_kernel,
        out_shape=jax.ShapeDtypeStruct((1, tokens, width), F32),
        in_specs=[pl.BlockSpec(memory_space=pltpu.VMEM)] * 12,
        out_specs=pl.BlockSpec(memory_space=pltpu.HBM),
        scratch_shapes=[pltpu.VMEM((tokens, width), F32), pltpu.SemaphoreType.DMA((2,))],
        compiler_params=pltpu.CompilerParams(vmem_limit_bytes=6 * 2**20),
        cost_estimate=pl.CostEstimate(flops=2 * 10**9, bytes_accessed=6 * 10**6, transcendentals=0),
    )(received, gr, dqt, dk, dv, *weights)


def finish_kernel(rank, count, *refs):
    ins, outs = refs[:count], refs[count : count + 8]
    scratch, singles, sems = refs[-6], refs[-5:-1], refs[-1]
    total = ins[0][...].astype(F32)
    for one in ins[1:]:
        total = total + one[...].astype(F32)
    scratch[...] = total
    copies = []
    for i, out in enumerate(outs):
        if i < 4:
            source = scratch.at[pl.ds(i * rank, rank)]
        else:
            source = singles[i - 4]
            source[...] = total[4 * rank + i - 4]
        copies.append(pltpu.make_async_copy(source, out, sems.at[i]))
    for copy in copies:
        copy.start()
    for copy in copies:
        copy.wait()


def call_finish(rank, parts):
    rows, width = parts[0].shape
    shape = jax.ShapeDtypeStruct
    return pl.pallas_call(
        functools.partial(finish_kernel, rank, len(parts)),
        out_shape=(shape((rank, width), F32),) * 4 + (shape((width,), F32),) * 4,
        in_specs=[pl.BlockSpec(memory_space=pltpu.VMEM)] * len(parts),
        out_specs=(pl.BlockSpec(memory_space=pltpu.HBM),) * 8,
        scratch_shapes=[pltpu.VMEM((rows, width), F32)]
        + [pltpu.VMEM((width,), F32)] * 4
        + [pltpu.SemaphoreType.DMA((8,))],
        compiler_params=pltpu.CompilerParams(vmem_limit_bytes=4 * 2**20),
    )(*parts)


def swapped(values, axis, partners):
    size = lax.axis_size(axis)
    return [values] + [
        lax.ppermute(values, axis, [(i, i ^ p) for i in range(size)]) for p in partners
    ]


def added(parts):
    total = parts[0].astype(F32)
    for one in parts[1:]:
        total = total + one.astype(F32)
    return total.astype(BF16)


def parts_of_sum(values, beside):
    parts = swapped(values, "seq", (1,))
    stride, size = 1, lax.axis_size("dp")
    while stride < size:
        radix = min(4, size // stride)
        parts = swapped(added(parts), "dp", [stride * k for k in range(1, radix)])
        if stride == 1:
            *parts, beside = lax.optimization_barrier((*parts, beside))
        stride *= radix
    return parts, beside


def body(
    inputs,
    pair_lengths,
    w_query,
    w_key,
    w_value,
    w_out,
    w_up,
    w_down,
    a_query,
    b_query,
    a_value,
    b_value,
    gain_one,
    shift_one,
    gain_two,
    shift_two,
    cotangent,
):
    rank = a_query.shape[1]
    swap = [(0, 1), (1, 0)]
    other = lax.ppermute(inputs, "seq", swap)
    lows = (a_query.T, b_query, a_value.T, b_value)
    gains = (gain_one, shift_one, gain_two, shift_two)
    *projected, wq, aqt = call_project(inputs, w_query, w_key, w_value, lows, w_out, w_up)
    wk, wv, bq, avt, bv = projected[8:13]
    output, gr, dqt, ds, dv, dv_halo, packed = call_layer(
        pair_lengths, projected, other, gains, w_up, w_down, cotangent
    )
    beside = call_keys(pair_lengths, projected[1], ds, dv_halo, wk, wv, avt, bv)
    parts, (dk, sent) = parts_of_sum(packed, beside)
    received = lax.ppermute(sent, "seq", swap)
    grad_inputs = call_inputs(received, gr, dqt, dk, dv, wq, wk, wv, aqt, bq, avt, bv)
    *parts, grad_inputs = lax.optimization_barrier((*parts, grad_inputs))
    gaq, gbq, gav, gbv, *norms = call_finish(rank, parts)
    return (output, grad_inputs, gaq.T, gbq, gav.T, gbv, *norms)


def solution(mesh):
    tokens = P("dp", "seq", None)
    in_specs = (tokens, P("dp", None)) + (P(),) * 14 + (tokens,)
    out_specs = (tokens, tokens) + (P(),) * 8
    return jax.shard_map(body, mesh=mesh, in_specs=in_specs, out_specs=out_specs, check_vma=False)
```

```python
import functools
import math

import jax
import jax.numpy as jnp
from jax import lax
from jax.experimental import pallas as pl
from jax.experimental.pallas import tpu as pltpu
from jax.sharding import PartitionSpec as P

DH = 64
LANES = 128
EDGE = 48
EARLY = 3
EPSILON = 1e-05
LOG2_E = math.log2(math.e)
FAR_AWAY = -1e30
BF16 = jnp.bfloat16
F32 = jnp.float32
NN = ((1,), (0,))
NT = ((1,), (1,))
TN = ((0,), (0,))
TT = ((0,), (1,))


def dot(former, latter, dims=NN):
    return lax.dot_general(former, latter, (dims, ((), ())), preferred_element_type=F32)


def normed(values):
    centred = values - jnp.mean(values, axis=-1, keepdims=True)
    variance = jnp.mean(centred * centred, axis=-1, keepdims=True)
    inverse = lax.rsqrt(variance + EPSILON)
    return centred * inverse, inverse


def norm_back(grad, normal, inverse):
    return inverse * (
        grad
        - jnp.mean(grad, axis=-1, keepdims=True)
        - normal * jnp.mean(grad * normal, axis=-1, keepdims=True)
    )


def gelu_and_slope(values):
    below = 0.5 + 0.5 * lax.erf(values * (1.0 / math.sqrt(2.0)))
    bell = jnp.exp2(values * values * (-0.5 * LOG2_E))
    return values * below, below + values * bell * (1.0 / math.sqrt(2.0 * math.pi))


def segment_codes(lengths_ref, start_near, start_far, rows):
    row = lax.broadcasted_iota(jnp.int32, (rows, LANES), 0)
    half = rows // 2
    place = jnp.where(row < half, start_near + row, start_far + row - half)
    segment = jnp.zeros_like(place)
    end = jnp.int32(0)
    for pair in range(lengths_ref.shape[1]):
        end = end + lengths_ref[0, pair]
        segment = segment + (place >= end).astype(jnp.int32)
    return segment


def crosses_widely(lengths_ref, middle, half):
    end = jnp.int32(0)
    left = jnp.int32(middle)
    right = jnp.int32(middle)
    for pair in range(lengths_ref.shape[1]):
        end = end + lengths_ref[0, pair]
        left = jnp.where(end < middle, middle - end, left)
        right = jnp.where(end >= middle, jnp.minimum(right, end - middle), right)
    return (right > 0) & ((left > half) | (right > half))


def edge_rows(side, half):
    return pl.multiple_of((1 - side) * (half - EDGE), 16)


def in_hbm(*arrays):
    return [pltpu.with_memory_space_constraint(a, pltpu.HBM) for a in arrays]


def own_rows(side, half):
    return pl.multiple_of((1 - side) * half, half), pl.multiple_of(side * half, half)


def project_kernel(
    x_hbm,
    wq_hbm,
    wk_hbm,
    wv_hbm,
    aqt_hbm,
    bq_hbm,
    avt_hbm,
    bv_hbm,
    wo_hbm,
    wu_hbm,
    x_ref,
    q_ref,
    k_ref,
    v_ref,
    kt_ref,
    vt_ref,
    qlow_ref,
    vlow_ref,
    wk,
    wv,
    bq,
    avt,
    bv,
    wo,
    wu,
    wq,
    aqt,
    sems,
):
    tokens = x_hbm.shape[1]
    half = tokens // 2
    near, far = own_rows(lax.axis_index("seq"), half)
    pairs = (
        (x_hbm.at[0, pl.ds(near, half)], x_ref.at[pl.ds(0, half)]),
        (x_hbm.at[0, pl.ds(far, half)], x_ref.at[pl.ds(half, half)]),
        (wk_hbm, wk),
        (aqt_hbm, aqt),
        (bq_hbm, bq),
        (avt_hbm, avt),
        (bv_hbm, bv),
        (wq_hbm, wq),
        (wv_hbm, wv),
        (wo_hbm, wo),
        (wu_hbm.at[:, pl.ds(0, wu.shape[1])], wu),
    )
    copies = [pltpu.make_async_copy(a, b, sems.at[i]) for i, (a, b) in enumerate(pairs)]
    for copy in copies:
        copy.start()
    for copy in copies[:3]:
        copy.wait()
    x = x_ref[...]
    keys = dot(x, wk[...]).astype(BF16)
    k_ref[...] = keys
    kt_ref[...] = keys.T
    for copy in copies[3:9]:
        copy.wait()
    qlow_t = dot(aqt[...], x, NT).astype(BF16)
    vlow_t = dot(avt[...], x, NT).astype(BF16)
    qlow_ref[...] = qlow_t
    vlow_ref[...] = vlow_t
    vals = (dot(x, wv[...]) + 2.0 * dot(vlow_t, bv[...], TN)).astype(BF16)
    v_ref[...] = vals
    vt_ref[...] = vals.T
    q_ref[...] = (
        (dot(x, wq[...]) + 2.0 * dot(qlow_t, bq[...], TN)) * (LOG2_E / math.sqrt(DH))
    ).astype(BF16)
    for copy in copies[9:]:
        copy.wait()


def call_project(x, wq, wk, wv, lows, wo, wu):
    _, tokens, width = x.shape
    rank = lows[1].shape[0]
    shape = jax.ShapeDtypeStruct
    rows, columns = shape((tokens, width), BF16), shape((width, tokens), BF16)
    low = shape((rank, tokens), BF16)
    square, flat = shape((width, width), BF16), shape((rank, width), BF16)
    return pl.pallas_call(
        project_kernel,
        out_shape=(rows,) * 4
        + (columns,) * 2
        + (low,) * 2
        + (square,) * 2
        + (flat,) * 3
        + (square, shape((width, EARLY * width), BF16), square, flat),
        in_specs=[pl.BlockSpec(memory_space=pltpu.HBM)] * 10,
        out_specs=(pl.BlockSpec(memory_space=pltpu.VMEM),) * 17,
        scratch_shapes=[pltpu.SemaphoreType.DMA((11,))],
        compiler_params=pltpu.CompilerParams(vmem_limit_bytes=20 * 2**20),
        cost_estimate=pl.CostEstimate(flops=10**9, bytes_accessed=8 * 10**6, transcendentals=0),
    )(*in_hbm(x, wq, wk, wv, *lows, wo, wu))


def layer_kernel(
    lengths_ref,
    x_ref,
    q_s,
    k_s,
    v_s,
    kt_s,
    vt_s,
    qlow_ref,
    vlow_ref,
    wk,
    wv,
    bq_ref,
    avt_ref,
    bv_ref,
    wo,
    wu_early,
    other_ref,
    gain_one_hbm,
    shift_one_hbm,
    gain_two_hbm,
    shift_two_hbm,
    wu_hbm,
    wd_hbm,
    cot_hbm,
    out_hbm,
    gr_s,
    dqt_s,
    ds_s,
    dv_s,
    halo_s,
    packed_ref,
    gain_one_s,
    shift_one_s,
    gain_two_s,
    shift_two_s,
    x_s,
    wu_late,
    wd,
    cot_s,
    kh_s,
    vh_s,
    kht_s,
    vht_s,
    p_s,
    inv_s,
    ct_s,
    normal_s,
    rstd_s,
    hidden_s,
    active_s,
    slope_s,
    total_s,
    out_s,
    dot_s,
    sems,
):
    tokens, width = x_ref.shape
    half = tokens // 2
    hidden = wu_hbm.shape[1]
    rank = bq_ref.shape[0]
    heads = width // DH
    side = lax.axis_index("seq")
    near, far = own_rows(side, half)

    copies = []

    def fetch(source, target):
        copy = pltpu.make_async_copy(source, target, sems.at[len(copies)])
        copies.append(copy)
        copy.start()
        return copy

    get_gains = [
        fetch(gain_one_hbm, gain_one_s),
        fetch(shift_one_hbm, shift_one_s),
        fetch(gain_two_hbm, gain_two_s),
        fetch(shift_two_hbm, shift_two_s),
    ]
    chunks = hidden // width
    early = wu_early.shape[1]
    get_ffn = [fetch(wu_hbm.at[:, pl.ds(early, hidden - early)], wu_late)]
    for c in range(chunks):
        part = pl.ds(c * width, width)
        get_ffn.append(fetch(wd_hbm.at[part], wd.at[part]))

    def wu_part(c):
        start = c * width
        if start < early:
            return wu_early[:, pl.ds(start, width)]
        return wu_late[:, pl.ds(start - early, width)]

    get_cot = [
        fetch(cot_hbm.at[0, pl.ds(near, half)], cot_s.at[pl.ds(0, half)]),
        fetch(cot_hbm.at[0, pl.ds(far, half)], cot_s.at[pl.ds(half, half)]),
    ]

    wide = crosses_widely(lengths_ref, tokens, half)
    own_segment = segment_codes(lengths_ref, side * tokens + near, side * tokens + far, tokens)
    halo_base = (1 - side) * tokens
    halo_segment = segment_codes(lengths_ref, halo_base + far, halo_base + near, tokens)
    lane = lax.broadcasted_iota(jnp.int32, (tokens, LANES), 1)
    code = lane & (DH - 1)
    low_lanes = lax.broadcasted_iota(jnp.int32, (2 * tokens, LANES), 1) < DH
    marks = lengths_ref.shape[1] + 1
    q_code = jnp.where(code == own_segment, 1.0, 0.0).astype(BF16)

    def key_code(segment):
        return jnp.where((code < marks) & (code != segment), FAR_AWAY, 0.0).astype(BF16)

    ko_code = key_code(own_segment)
    kh_code = key_code(halo_segment)

    bq, avt, bv = bq_ref[...], avt_ref[...], bv_ref[...]
    qlow_t, vlow_t = qlow_ref[...], vlow_ref[...]
    x_s[pl.ds(0, half)] = other_ref[0, pl.ds(far, half)]
    x_s[pl.ds(half, half)] = other_ref[0, pl.ds(near, half)]
    halo_low_t = dot(avt, x_s[...], NT).astype(BF16)

    def project_halo(start):
        rows = pl.ds(start, half)
        x_halo = x_s[rows]
        keys = dot(x_halo, wk[...]).astype(BF16)
        kh_s[rows] = keys
        kht_s[:, rows] = keys.T
        low_t = halo_low_t[:, start : start + half]
        vals = (dot(x_halo, wv[...]) + 2.0 * dot(low_t, bv, TN)).astype(BF16)
        vh_s[rows] = vals
        vht_s[:, rows] = vals.T

    def joined(own, halo, reach, join):
        if reach == tokens:
            return join(own, halo)
        return jnp.concatenate([join(own[:, :reach], halo), own[:, reach:]], axis=1)

    def lanes_of(pair):
        return pl.ds(pl.multiple_of(pair * LANES, LANES), LANES)

    def rows_of(pair, odd):
        return pl.ds(pl.multiple_of(pair * LANES + odd * DH, DH), DH)

    def score(pair, odd, reach):
        lanes = lanes_of(pair)

        def mixed(values, codes):
            mask = low_lanes[: values.shape[0]]
            if odd:
                return jnp.where(mask, codes, values)
            return jnp.where(mask, values, codes)

        k_pair = jnp.concatenate([k_s[:, lanes], kh_s[pl.ds(0, reach), lanes]], axis=0)
        k_code = jnp.concatenate([ko_code, kh_code[:reach]], axis=0)
        return dot(mixed(k_pair, k_code), mixed(q_s[:, lanes], q_code), NT)

    def soften(pair, odd, reach, scores):
        head = 2 * pair + odd
        own, halo = scores[:tokens], scores[tokens:, :reach]
        peak = joined(
            jnp.max(own, axis=0, keepdims=True),
            jnp.max(halo, axis=0, keepdims=True),
            reach,
            jnp.maximum,
        )
        own = jnp.exp2(own - peak)
        halo = jnp.exp2(halo - peak[:, :reach])
        inverse = 1.0 / joined(
            jnp.sum(own, axis=0, keepdims=True),
            jnp.sum(halo, axis=0, keepdims=True),
            reach,
            jnp.add,
        )
        own, halo = own.astype(BF16), halo.astype(BF16)
        p_s[head, pl.ds(0, tokens)] = own
        p_s[head, pl.ds(tokens, reach), pl.ds(0, reach)] = halo
        inv_s[head] = jnp.broadcast_to(inverse, inv_s.shape[1:])
        return own, halo, inverse

    def attend(pair, odd, reach, soft):
        own, halo, inverse = soft
        rows = rows_of(pair, odd)
        context = joined(
            dot(vt_s[rows, :], own),
            dot(vht_s[rows, pl.ds(0, reach)], halo),
            reach,
            jnp.add,
        )
        ct_s[rows, :] = (context * inverse).astype(BF16)

    def back_score(pair, odd, reach):
        lanes = lanes_of(pair)
        inverse = inv_s[2 * pair + odd, pl.ds(0, 1), :]
        grad = (dot_s[rows_of(pair, odd), :] * inverse).astype(BF16)
        blank = jnp.zeros_like(grad)
        grad = jnp.concatenate([blank, grad] if odd else [grad, blank], axis=0)
        own = dot(v_s[:, lanes], grad)
        halo = dot(vh_s[pl.ds(0, reach), lanes], grad[:, :reach])
        return inverse, grad, own, halo

    evens = {}

    def back_soften(pair, odd, reach, slopes):
        head = 2 * pair + odd
        inverse, grad, own, halo = slopes
        p_own, p_halo = p_s[head, pl.ds(0, tokens)], p_s[head, pl.ds(tokens, reach), pl.ds(0, reach)]
        po, ph = p_own.astype(F32), p_halo.astype(F32)
        own, halo = po * own, ph * halo
        inner = inverse * joined(
            jnp.sum(own, axis=0, keepdims=True),
            jnp.sum(halo, axis=0, keepdims=True),
            reach,
            jnp.add,
        )
        own = (own - po * inner).astype(BF16)
        halo = (halo - ph * inner[:, :reach]).astype(BF16)
        ds_s[head, pl.ds(0, tokens)] = own
        ds_s[head, pl.ds(tokens, reach), pl.ds(0, reach)] = halo
        return grad, p_own, p_halo, own, halo

    def attend_back(pair, odd, reach, soft):
        lanes, rows = lanes_of(pair), rows_of(pair, odd)
        grad, p_own, p_halo, own, halo = soft
        parts = (dot(p_own, grad, NT), dot(p_halo, grad[:, :reach], NT))
        dq = joined(
            dot(kt_s[rows, :], own),
            dot(kht_s[rows, pl.ds(0, reach)], halo),
            reach,
            jnp.add,
        )
        dqt_s[rows, :] = (dq * (1.0 / math.sqrt(DH))).astype(BF16)
        if not odd:
            evens[0] = parts
            return
        even = evens.pop(0)
        dv_s[:, lanes] = (even[0] + parts[0]).astype(BF16)
        halo_s[pl.ds(0, reach), lanes] = (even[1] + parts[1]).astype(BF16)

    def for_heads(reach, first, second, third, lags):
        if reach == tokens:

            def step(pair, none):
                for odd in range(2):
                    soft = second(pair, odd, tokens, first(pair, odd, tokens))
                    third(pair, odd, tokens, soft)

            lax.fori_loop(0, heads // 2, step, None)
            return
        todo = [(pair, odd) for pair in range(heads // 2) for odd in range(2)]
        one, two = {}, {}
        for at in range(len(todo) + lags[1]):
            if at < len(todo):
                one[at] = first(*todo[at], reach)
            back = at - lags[0]
            if 0 <= back < len(todo):
                two[back] = second(*todo[back], reach, one.pop(back))
            back = at - lags[1]
            if 0 <= back:
                third(*todo[back], reach, two.pop(back))

    def run(reach):
        project_halo(0)
        if reach == tokens:
            project_halo(half)
        for_heads(reach, score, soften, attend, (2, 4))

        for copy in get_gains:
            copy.wait()
        resid_one = x_ref[...].astype(F32) + dot(ct_s[...], wo[...], TN)
        normal, inverse = normed(resid_one)
        normal_s[...] = normal
        rstd_s[...] = jnp.broadcast_to(inverse, rstd_s.shape)
        gain_one, shift_one = gain_one_s[...].reshape(1, width), shift_one_s[...].reshape(1, width)
        gain_two, shift_two = gain_two_s[...].reshape(1, width), shift_two_s[...].reshape(1, width)
        hidden_one = normal * gain_one + shift_one
        hidden_s[...] = hidden_one.astype(BF16)
        total_s[...] = hidden_one
        for copy in get_ffn:
            copy.wait()
        upward = dot(hidden_s[...], wu_part(0))
        for c in range(chunks):
            part = pl.ds(c * width, width)
            ahead = dot(hidden_s[...], wu_part(c + 1)) if c + 1 < chunks else None
            value, slope = gelu_and_slope(upward)
            active_s[:, part] = value.astype(BF16)
            slope_s[:, part] = slope.astype(BF16)
            total_s[...] += dot(active_s[:, part], wd[part, :])
            upward = ahead
        normal_two, inverse_two = normed(total_s[...])
        out_s[...] = (normal_two * gain_two + shift_two).astype(BF16)

        def put(source, target):
            return fetch(source, target)

        puts = [
            put(out_s.at[pl.ds(0, half)], out_hbm.at[0, pl.ds(near, half)]),
            put(out_s.at[pl.ds(half, half)], out_hbm.at[0, pl.ds(far, half)]),
        ]
        for copy in get_cot:
            copy.wait()
        grad_out = cot_s[...].astype(F32)
        grad_gain_two = jnp.sum(grad_out * normal_two, axis=0, keepdims=True)
        grad_shift_two = jnp.sum(grad_out, axis=0, keepdims=True)
        grad_two = norm_back(grad_out * gain_two, normal_two, inverse_two)
        hidden_s[...] = grad_two.astype(BF16)
        total_s[...] = grad_two
        grad_active = dot(hidden_s[...], wd[pl.ds(0, width), :], NT)
        for c in range(chunks):
            part = pl.ds(c * width, width)
            ahead = None
            if c + 1 < chunks:
                ahead = dot(hidden_s[...], wd[pl.ds((c + 1) * width, width), :], NT)
            active_s[:, part] = (slope_s[:, part].astype(F32) * grad_active).astype(BF16)
            total_s[...] += dot(active_s[:, part], wu_part(c), NT)
            grad_active = ahead
        grad_hidden = total_s[...]
        normal = normal_s[...]
        grad_gain_one = jnp.sum(grad_hidden * normal, axis=0, keepdims=True)
        grad_shift_one = jnp.sum(grad_hidden, axis=0, keepdims=True)
        grad_one = norm_back(grad_hidden * gain_one, normal, rstd_s[:, :1])
        gr_s[...] = grad_one
        dot_s[...] = dot(wo[...], grad_one.astype(BF16), NT)

        if reach < tokens:
            halo_s[pl.ds(half, half)] = jnp.zeros((half, width), BF16)

        for_heads(reach, back_score, back_soften, attend_back, (2, 4))

        dv_halo = halo_s[pl.ds(0, reach)]
        x_own = x_ref[...]
        grad_qlow_t = (2.0 * dot(bq, dqt_s[...])).astype(BF16)
        grad_vlow_t = (2.0 * dot(bv, dv_s[...], NT)).astype(BF16)
        grad_halo_t = (2.0 * dot(bv, dv_halo, NT)).astype(BF16)
        rows = [
            dot(grad_qlow_t, x_own),
            2.0 * dot(qlow_t, dqt_s[...], NT),
            dot(grad_vlow_t, x_own) + dot(grad_halo_t, x_s[pl.ds(0, reach)]),
            2.0 * (dot(vlow_t, dv_s[...]) + dot(halo_low_t[:, :reach], dv_halo)),
            grad_gain_one,
            grad_shift_one,
            grad_gain_two,
            grad_shift_two,
        ]
        spare = packed_ref.shape[0] - 4 * rank - 4
        rows.append(jnp.zeros((spare, width), F32))
        packed_ref[...] = jnp.concatenate(rows, axis=0).astype(BF16)
        for copy in puts:
            copy.wait()

    @pl.when(jnp.logical_not(wide))
    def _():
        run(half)

    @pl.when(wide)
    def _():
        run(tokens)


def call_layer(lengths, projected, other, gains, wu, wd, cotangent):
    _, tokens, width = other.shape
    hidden = wu.shape[1]
    heads = width // DH
    rank = projected[6].shape[0]
    packed_rows = -(-(4 * rank + 4) // 8) * 8
    hbm = pl.BlockSpec(memory_space=pltpu.HBM)
    here = pl.BlockSpec(memory_space=pltpu.VMEM)
    shape = jax.ShapeDtypeStruct
    vmem = pltpu.VMEM
    return pl.pallas_call(
        layer_kernel,
        out_shape=(
            shape((1, tokens, width), BF16),
            shape((tokens, width), F32),
            shape((width, tokens), BF16),
            shape((heads, 2 * tokens, tokens), BF16),
            shape((tokens, width), BF16),
            shape((tokens, width), BF16),
            shape((packed_rows, width), BF16),
        ),
        in_specs=[pl.BlockSpec(memory_space=pltpu.SMEM)] + [here] * 16 + [hbm] * 7,
        out_specs=(hbm,) + (here,) * 6,
        scratch_shapes=[
            vmem((width,), F32),
            vmem((width,), F32),
            vmem((width,), F32),
            vmem((width,), F32),
            vmem((tokens, width), BF16),
            vmem((width, hidden - EARLY * width), BF16),
            vmem(wd.shape, BF16),
            vmem((tokens, width), BF16),
            vmem((tokens, width), BF16),
            vmem((tokens, width), BF16),
            vmem((width, tokens), BF16),
            vmem((width, tokens), BF16),
            vmem((heads, 2 * tokens, tokens), BF16),
            vmem((heads, 8, tokens), F32),
            vmem((width, tokens), BF16),
            vmem((tokens, width), F32),
            vmem((tokens, LANES), F32),
            vmem((tokens, width), BF16),
            vmem((tokens, hidden), BF16),
            vmem((tokens, hidden), BF16),
            vmem((tokens, width), F32),
            vmem((tokens, width), BF16),
            vmem((width, tokens), F32),
            pltpu.SemaphoreType.DMA((32,)),
        ],
        compiler_params=pltpu.CompilerParams(vmem_limit_bytes=36 * 2**20),
        cost_estimate=pl.CostEstimate(flops=9 * 10**9, bytes_accessed=15 * 10**6, transcendentals=0),
    )(lengths, *projected, other, *in_hbm(*gains, wu, wd, cotangent))


def keys_kernel(
    lengths_ref,
    q_ref,
    ds_ref,
    dv_ref,
    wk,
    wv,
    avt,
    bv,
    dk_ref,
    sent_ref,
    halo_s,
):
    tokens, width = q_ref.shape
    half = tokens // 2
    wide = crosses_widely(lengths_ref, tokens, half)
    low_lanes = lax.broadcasted_iota(jnp.int32, (tokens, LANES), 1) < DH
    unscale = 1.0 / LOG2_E

    def step(pair, reach):
        lanes = pl.ds(pl.multiple_of(pair * LANES, LANES), LANES)
        q_pair = q_ref[:, lanes]
        own = [dot(ds_ref[2 * pair + odd, pl.ds(0, tokens)], q_pair) for odd in range(2)]
        halo = [
            dot(ds_ref[2 * pair + odd, pl.ds(tokens, reach), pl.ds(0, reach)], q_pair[:reach])
            for odd in range(2)
        ]
        dk_ref[:, lanes] = (jnp.where(low_lanes, *own) * unscale).astype(BF16)
        halo_s[pl.ds(0, reach), lanes] = (
            jnp.where(low_lanes[:reach], *halo) * unscale
        ).astype(BF16)

    def send(rows, target):
        grad_v = dv_ref[rows]
        low_t = (2.0 * dot(bv[...], grad_v, NT)).astype(BF16)
        sent_ref[target] = (
            dot(halo_s[rows], wk[...], NT) + dot(grad_v, wv[...], NT) + dot(low_t, avt[...], TN)
        ).astype(BF16)

    @pl.when(jnp.logical_not(wide))
    def _():
        for pair in range(width // LANES):
            step(pair, half)

    @pl.when(wide)
    def _():
        lax.fori_loop(0, width // LANES, lambda pair, none: step(pair, tokens), None)

    send(pl.ds(0, half), pl.ds(0, half))

    @pl.when(jnp.logical_not(wide))
    def _():
        sent_ref[pl.ds(half, EDGE)] = jnp.zeros((EDGE, width), BF16)

    @pl.when(wide)
    def _():
        other = 1 - lax.axis_index("seq")
        send(pl.ds(half + edge_rows(other, half), EDGE), pl.ds(half, EDGE))


def call_keys(lengths, q, ds, dv_halo, wk, wv, avt, bv):
    tokens, width = q.shape
    rows = jax.ShapeDtypeStruct((tokens, width), BF16)
    return pl.pallas_call(
        keys_kernel,
        out_shape=(rows, jax.ShapeDtypeStruct((tokens // 2 + EDGE, width), BF16)),
        in_specs=[pl.BlockSpec(memory_space=pltpu.SMEM)]
        + [pl.BlockSpec(memory_space=pltpu.VMEM)] * 7,
        out_specs=(pl.BlockSpec(memory_space=pltpu.VMEM),) * 2,
        scratch_shapes=[pltpu.VMEM((tokens, width), BF16)],
        compiler_params=pltpu.CompilerParams(vmem_limit_bytes=6 * 2**20),
        cost_estimate=pl.CostEstimate(flops=2 * 10**9, bytes_accessed=6 * 10**6, transcendentals=0),
    )(lengths, q, ds, dv_halo, wk, wv, avt, bv)


def inputs_kernel(
    received_ref,
    gr,
    dqt,
    dk,
    dv,
    wq,
    wk,
    wv,
    aqt,
    bq,
    avt,
    bv,
    out_hbm,
    out_s,
    sems,
):
    tokens, width = gr.shape
    half = tokens // 2
    side = lax.axis_index("seq")
    near, far = own_rows(side, half)
    grad_qlow_t = (2.0 * dot(bq[...], dqt[...])).astype(BF16)
    grad_vlow_t = (2.0 * dot(bv[...], dv[...], NT)).astype(BF16)
    out_s[...] = (
        gr[...]
        + dot(dk[...], wk[...], NT)
        + dot(dv[...], wv[...], NT)
        + dot(dqt[...], wq[...], TT)
        + dot(grad_qlow_t, aqt[...], TN)
        + dot(grad_vlow_t, avt[...], TN)
    )
    out_s[pl.ds(0, half)] += received_ref[pl.ds(0, half)].astype(F32)
    edge = pl.ds(half + edge_rows(side, half), EDGE)
    out_s[edge] += received_ref[pl.ds(half, EDGE)].astype(F32)
    puts = [
        pltpu.make_async_copy(
            out_s.at[pl.ds(0, half)], out_hbm.at[0, pl.ds(near, half)], sems.at[0]
        ),
        pltpu.make_async_copy(
            out_s.at[pl.ds(half, half)], out_hbm.at[0, pl.ds(far, half)], sems.at[1]
        ),
    ]
    for copy in puts:
        copy.start()
    for copy in puts:
        copy.wait()


def call_inputs(received, gr, dqt, dk, dv, *weights):
    tokens, width = gr.shape
    return pl.pallas_call(
        inputs_kernel,
        out_shape=jax.ShapeDtypeStruct((1, tokens, width), F32),
        in_specs=[pl.BlockSpec(memory_space=pltpu.VMEM)] * 12,
        out_specs=pl.BlockSpec(memory_space=pltpu.HBM),
        scratch_shapes=[pltpu.VMEM((tokens, width), F32), pltpu.SemaphoreType.DMA((2,))],
        compiler_params=pltpu.CompilerParams(vmem_limit_bytes=6 * 2**20),
        cost_estimate=pl.CostEstimate(flops=2 * 10**9, bytes_accessed=6 * 10**6, transcendentals=0),
    )(received, gr, dqt, dk, dv, *weights)


def finish_kernel(rank, count, *refs):
    ins, outs = refs[:count], refs[count : count + 8]
    scratch, singles, sems = refs[-6], refs[-5:-1], refs[-1]
    total = ins[0][...].astype(F32)
    for one in ins[1:]:
        total = total + one[...].astype(F32)
    scratch[...] = total
    copies = []
    for i, out in enumerate(outs):
        if i < 4:
            source = scratch.at[pl.ds(i * rank, rank)]
        else:
            source = singles[i - 4]
            source[...] = total[4 * rank + i - 4]
        copies.append(pltpu.make_async_copy(source, out, sems.at[i]))
    for copy in copies:
        copy.start()
    for copy in copies:
        copy.wait()


def call_finish(rank, parts):
    rows, width = parts[0].shape
    shape = jax.ShapeDtypeStruct
    return pl.pallas_call(
        functools.partial(finish_kernel, rank, len(parts)),
        out_shape=(shape((rank, width), F32),) * 4 + (shape((width,), F32),) * 4,
        in_specs=[pl.BlockSpec(memory_space=pltpu.VMEM)] * len(parts),
        out_specs=(pl.BlockSpec(memory_space=pltpu.HBM),) * 8,
        scratch_shapes=[pltpu.VMEM((rows, width), F32)]
        + [pltpu.VMEM((width,), F32)] * 4
        + [pltpu.SemaphoreType.DMA((8,))],
        compiler_params=pltpu.CompilerParams(vmem_limit_bytes=4 * 2**20),
    )(*parts)


def swapped(values, axis, partners):
    size = lax.axis_size(axis)
    return [values] + [
        lax.ppermute(values, axis, [(i, i ^ p) for i in range(size)]) for p in partners
    ]


def added(parts):
    total = parts[0].astype(F32)
    for one in parts[1:]:
        total = total + one.astype(F32)
    return total.astype(BF16)


def parts_of_sum(values, beside):
    parts = swapped(values, "seq", (1,))
    stride, size = 1, lax.axis_size("dp")
    while stride < size:
        radix = min(4, size // stride)
        parts = swapped(added(parts), "dp", [stride * k for k in range(1, radix)])
        if stride == 1:
            *parts, beside = lax.optimization_barrier((*parts, beside))
        stride *= radix
    return parts, beside


def body(
    inputs,
    pair_lengths,
    w_query,
    w_key,
    w_value,
    w_out,
    w_up,
    w_down,
    a_query,
    b_query,
    a_value,
    b_value,
    gain_one,
    shift_one,
    gain_two,
    shift_two,
    cotangent,
):
    rank = a_query.shape[1]
    swap = [(0, 1), (1, 0)]
    other = lax.ppermute(inputs, "seq", swap)
    lows = (a_query.T, b_query, a_value.T, b_value)
    gains = (gain_one, shift_one, gain_two, shift_two)
    *projected, wq, aqt = call_project(inputs, w_query, w_key, w_value, lows, w_out, w_up)
    wk, wv, bq, avt, bv = projected[8:13]
    output, gr, dqt, ds, dv, dv_halo, packed = call_layer(
        pair_lengths, projected, other, gains, w_up, w_down, cotangent
    )
    beside = call_keys(pair_lengths, projected[1], ds, dv_halo, wk, wv, avt, bv)
    parts, (dk, sent) = parts_of_sum(packed, beside)
    received = lax.ppermute(sent, "seq", swap)
    grad_inputs = call_inputs(received, gr, dqt, dk, dv, wq, wk, wv, aqt, bq, avt, bv)
    *parts, grad_inputs = lax.optimization_barrier((*parts, grad_inputs))
    gaq, gbq, gav, gbv, *norms = call_finish(rank, parts)
    return (output, grad_inputs, gaq.T, gbq, gav.T, gbv, *norms)


def solution(mesh):
    tokens = P("dp", "seq", None)
    in_specs = (tokens, P("dp", None)) + (P(),) * 14 + (tokens,)
    out_specs = (tokens, tokens) + (P(),) * 8
    return jax.shard_map(body, mesh=mesh, in_specs=in_specs, out_specs=out_specs, check_vma=False)
```
